256 devices in a mesh: gx: 4 (over y), gy: 64 (over x, z, core).
Axes of the slice: x: 4, y: 4, z: 8, core: 2. Of those that a mesh axis runs over, the one named last changes fastest.
Arguments:
- hidden: bfloat16 [512, 2, 16384], P('gy', None, 'gx'), may hold values from -6 to 6
- norm_gain: bfloat16 [16384], P('gx'), may hold values from 0.5 to 1.5
- w_query: bfloat16 [16384, 16384], P('gx', 'gy'), may hold values from -0.046875 to 0.046875
- w_keyval: bfloat16 [2, 16384, 1024], P(None, 'gx', 'gy'), may hold values from -0.046875 to 0.046875
- w_out: bfloat16 [16384, 16384], P('gy', 'gx'), may hold values from -0.046875 to 0.046875
- cache_keys: bfloat16 [512, 1024, 1024], P(('gx', 'gy')), may hold values from -80 to 80, as said below
- cache_values: bfloat16 [512, 1024, 1024], P(('gx', 'gy')), may hold values from -16 to 16
- cache_lengths: int32 [512], P(('gx', 'gy')), may hold values from 1 to 1024, as said below
- positions: int32 [512], P(('gx', 'gy')), may hold values from 1 to 5119, as said below
Outputs:
- attn_branch: bfloat16 [512, 2, 16384], P('gy', None, 'gx')
- new_keyvals: bfloat16 [2, 512, 2, 1024], P(None, ('gx', 'gy'))
The draws below stay inside these ranges and needn't reach their ends.
Inputs may be any that keep to these rules, and one draw needn't show every extreme that they name: `cache_keys`: cached keys already carry their rotation. `cache_lengths`: some row has exactly 1024 valid slots and some row exactly 1. `positions`: each row's position is at least its cache length.
All inputs are finite; a program needn't handle non-finite values.
Results may differ from the reference program's by a relative error of at most 0.008.
The reference program's roundings to bfloat16 on the way count: a program that leaves them out, or rounds other values in their place, can miss the bound.
Values may be sent and summed in bfloat16 or wider, within the bound.
No kernel may reach another device: no remote copies, remote signals or barrier semaphores. Data moves between devices by JAX's collectives and lax.ppermute only.
A program may use at most 128 MiB of HBM per device.

```python
import math
import jax
import jax.numpy as jnp
from jax import lax

D = 16384
HQ = 128
KVH = 8
HD = 128
STEPS = 2
S = 1024
B = 512


def row_draw(key):
    count_key, pick_key = jax.random.split(key)
    lengths = jax.random.randint(count_key, (B,), 1, S + 1)
    order = jax.random.permutation(pick_key, B)
    lengths = lengths.at[order[0]].set(S).at[order[1]].set(1)
    return (lengths.astype(jnp.int32), order)


def draw_cache_lengths(key, part):
    lengths, order = row_draw(key)
    return lengths


def draw_positions(key, part):
    lengths, order = row_draw(key)
    key = jax.random.fold_in(key, 7)
    offsets = jax.random.randint(key, (B,), 0, 4 * S)
    offsets = offsets.at[order[0]].set(4 * S - 1).at[order[1]].set(0)
    return (lengths + offsets).astype(jnp.int32)


def draw_cache_keys(key, part):
    lengths, order = row_draw(key)
    key = jax.random.fold_in(key, 11)
    noise_key = jax.random.fold_in(key, 0)
    sign_key = jax.random.fold_in(key, 2)
    slot_key = jax.random.fold_in(key, 3)
    level_key = jax.random.fold_in(key, 4)
    base = jnp.clip(jax.random.normal(noise_key, (B, S, KVH * HD), jnp.float32) * 1.5, -9.0, 9.0)
    row_rank = jnp.zeros((B,), jnp.int32).at[order].set(jnp.arange(B, dtype=jnp.int32))
    strong_rows = (row_rank == 0) | (row_rank >= 2) & (row_rank < 2 + B // 8)
    level_table = jnp.array([40.0, 60.0, 80.0], jnp.float32)
    strength = level_table[jax.random.randint(level_key, (B,), 0, 3)]
    strength = jnp.where(row_rank == 0, 80.0, strength)
    sign_pattern = (jax.random.randint(sign_key, (B, KVH * HD), 0, 2) * 2 - 1).astype(jnp.float32)
    first_slot = jax.random.randint(slot_key, (B,), 0, lengths)
    second_slot = (first_slot + 1) % lengths
    rows_index = jnp.arange(B)
    keep_second = base[rows_index, second_slot]
    new_second = jnp.where(strong_rows[:, None], 0.985 * strength[:, None] * sign_pattern, keep_second)
    base = base.at[rows_index, second_slot].set(new_second)
    keep_first = base[rows_index, first_slot]
    new_first = jnp.where(strong_rows[:, None], strength[:, None] * sign_pattern, keep_first)
    base = base.at[rows_index, first_slot].set(new_first)
    return base.astype(jnp.bfloat16)


def shard_levels(key, extent, cuts, smallest, largest):
    level, own = 1.0, jax.random.fold_in(key, 6)
    for position, blocks in cuts:
        draws = jnp.exp(jax.random.uniform(jax.random.fold_in(own, position), (blocks,), jnp.float32, smallest / len(cuts), largest / len(cuts)))
        level = level * jnp.repeat(draws, extent[position] // blocks).reshape([-1 if axis == position else 1 for axis in range(len(extent))])
    return level


def gaussian(key, dims, spread, limit, cuts=(), held_as=jnp.bfloat16):
    values = spread * jax.random.normal(key, dims, jnp.float32)
    if cuts:
        values = values * shard_levels(key, dims, cuts, -0.22, 0.18)
    return jnp.clip(values, -limit, limit).astype(held_as)


def setup_inputs(seed: int = 0) -> dict:
    arg_keys = jax.random.split(jax.random.key(seed), 10)
    return {
        "hidden": gaussian(arg_keys[0], (B, STEPS, D), 1.0, 6.0, ((0, 64), (2, 4))),
        "norm_gain": jnp.clip(1.0 + 0.1 * jax.random.normal(arg_keys[1], (D,), jnp.float32), 0.5, 1.5).astype(jnp.bfloat16),
        "w_query": gaussian(arg_keys[2], (D, HQ * HD), D ** -0.5, 0.046875, ((0, 4), (1, 64))),
        "w_keyval": gaussian(arg_keys[3], (2, D, KVH * HD), D ** -0.5, 0.046875, ((1, 4), (2, 64))),
        "w_out": gaussian(arg_keys[4], (HQ * HD, D), (HQ * HD) ** -0.5, 0.046875, ((0, 64), (1, 4))),
        "cache_keys": draw_cache_keys(jax.random.fold_in(arg_keys[9], 71), 0),
        "cache_values": gaussian(arg_keys[6], (B, S, KVH * HD), 4.0, 16.0, ((0, 256),)),
        "cache_lengths": draw_cache_lengths(jax.random.fold_in(arg_keys[9], 71), 0),
        "positions": draw_positions(jax.random.fold_in(arg_keys[9], 71), 0),
    }


norm_epsilon = 1e-05

def rope_rates():
    index = jnp.arange(HD // 2, dtype=jnp.float32)
    rates = 1.0 / jnp.power(500000.0, 2.0 * index / HD)
    wavelength = 2.0 * math.pi / rates
    smooth = (8192.0 / wavelength - 1.0) / 3.0
    blended = (1.0 - smooth) * rates / 8.0 + smooth * rates
    return jnp.where(wavelength > 8192.0, rates / 8.0, jnp.where(wavelength < 2048.0, rates, blended))

def rotate(vectors, places):
    angles = places[..., None, None] * rope_rates()
    half_size = vectors.shape[-1] // 2
    first_half = vectors[..., :half_size]
    second_half = vectors[..., half_size:]
    cosine = jnp.cos(angles)
    sine = jnp.sin(angles)
    return jnp.concatenate([first_half * cosine - second_half * sine, second_half * cosine + first_half * sine], axis=-1)

def attend(queries, fresh_keys, fresh_values, cached_keys, cached_values, lengths):
    rows, steps = (queries.shape[0], queries.shape[1])
    slots = cached_keys.shape[1]
    grouped = queries.reshape(rows, steps, KVH, HQ // KVH, HD).astype(jnp.float32)
    old_keys = cached_keys.reshape(rows, slots, KVH, HD).astype(jnp.float32)
    old_values = cached_values.reshape(rows, slots, KVH, HD).astype(jnp.float32)
    score_scale = HD ** (-0.5)
    cached = jnp.einsum('bskgd,btkd->bskgt', grouped, old_keys) * score_scale
    fresh = jnp.einsum('bskgd,brkd->bskgr', grouped, fresh_keys.astype(jnp.float32)) * score_scale
    slot_valid = jnp.arange(slots)[None, :] < lengths[:, None]
    step_valid = jnp.arange(steps)[None, :] <= jnp.arange(steps)[:, None]
    cached = jnp.where(slot_valid[:, None, None, None, :], cached, -1e+30)
    fresh = jnp.where(step_valid[None, :, None, None, :], fresh, -1e+30)
    highest = jnp.maximum(lax.optimization_barrier(jnp.max(cached, axis=-1)), lax.optimization_barrier(jnp.max(fresh, axis=-1)))[..., None]
    weights_old = jnp.exp(cached - highest)
    weights_new = jnp.exp(fresh - highest)
    denom = lax.optimization_barrier(jnp.sum(weights_old, axis=-1)) + lax.optimization_barrier(jnp.sum(weights_new, axis=-1))
    rounded_old = weights_old.astype(jnp.bfloat16).astype(jnp.float32)
    rounded_new = weights_new.astype(jnp.bfloat16).astype(jnp.float32)
    mixed = jnp.einsum('bskgt,btkd->bskgd', rounded_old, old_values)
    mixed = mixed + jnp.einsum('bskgr,brkd->bskgd', rounded_new, fresh_values.astype(jnp.float32))
    return (mixed / denom[..., None]).astype(jnp.bfloat16).reshape(rows, steps, HQ * HD)

def one_row(items):
    outcome = attend(items[0][None], items[1][None], items[2][None], items[3][None], items[4][None], items[5][None])
    return outcome[0]

def reference(hidden, norm_gain, w_query, w_keyval, w_out, cache_keys, cache_values, cache_lengths, positions):
    features = hidden.astype(jnp.float32)
    mean_square = lax.optimization_barrier(jnp.mean(features * features, axis=-1, keepdims=True))
    normed = (features * lax.rsqrt(mean_square + norm_epsilon) * norm_gain.astype(jnp.float32)).astype(jnp.bfloat16)
    rows, steps = (hidden.shape[0], hidden.shape[1])
    flattened = normed.reshape(rows * steps, D)
    queries = jnp.dot(flattened, w_query, preferred_element_type=jnp.float32).astype(jnp.bfloat16).reshape(rows, steps, HQ, HD)
    fresh_keys = jnp.dot(flattened, w_keyval[0], preferred_element_type=jnp.float32).astype(jnp.bfloat16).reshape(rows, steps, KVH, HD)
    fresh_values = jnp.dot(flattened, w_keyval[1], preferred_element_type=jnp.float32).astype(jnp.bfloat16).reshape(rows, steps, KVH, HD)
    places = positions.astype(jnp.float32)[:, None] + jnp.arange(steps, dtype=jnp.float32)[None, :]
    turned_queries = rotate(queries.astype(jnp.float32), places).astype(jnp.bfloat16)
    turned_keys = rotate(fresh_keys.astype(jnp.float32), places).astype(jnp.bfloat16)
    new_keyvals = jnp.stack([turned_keys.reshape(rows, steps, KVH * HD), fresh_values.reshape(rows, steps, KVH * HD)])
    attended = lax.map(one_row, (turned_queries, turned_keys, fresh_values, cache_keys, cache_values, cache_lengths))
    branch = jnp.dot(attended.reshape(rows * steps, HQ * HD), w_out, preferred_element_type=jnp.float32)
    return (branch.reshape(rows, steps, D).astype(jnp.bfloat16), new_keyvals)
```

```python
import math

import jax
import jax.numpy as jnp
from jax import lax
from jax.experimental import pallas as pl
from jax.experimental.pallas import tpu as pltpu
from jax.sharding import Mesh
from jax.sharding import PartitionSpec as P

HQ = 128
KVH = 8
HD = 128
HALF = HD // 2
TOKENS = 4
NX, NY, NZ, NC = 4, 4, 8, 2
f32 = jnp.float32
bf16 = jnp.bfloat16

norm_epsilon = 1e-05


def rope_rates():
    index = jnp.arange(HD // 2, dtype=jnp.float32)
    rates = 1.0 / jnp.power(500000.0, 2.0 * index / HD)
    wavelength = 2.0 * math.pi / rates
    smooth = (8192.0 / wavelength - 1.0) / 3.0
    blended = (1.0 - smooth) * rates / 8.0 + smooth * rates
    return jnp.where(
        wavelength > 8192.0, rates / 8.0, jnp.where(wavelength < 2048.0, rates, blended)
    )


def recv(block, axis, distance):
    size = lax.axis_size(axis)
    return lax.ppermute(block, axis, [((i + distance) % size, i) for i in range(size)])


def roll_to(blocks, start):
    return lax.dynamic_slice_in_dim(
        jnp.concatenate([blocks, blocks], axis=0), start, blocks.shape[0], 0
    )


def dot(a, b):
    return jnp.dot(a, b, preferred_element_type=f32)


def attention_kernel(lengths, q, cosine, sine, k_old, v_old, k_new, v_new, out):
    queries = q[...].astype(f32)
    turned = (queries * cosine[...] + pltpu.roll(queries, HALF, 1) * sine[...]).astype(bf16)
    rows = turned.shape[0]
    slots = k_old.shape[1]
    contract_last = (((1,), (1,)), ((), ()))
    score_scale = HD ** (-0.5)

    def scores(keys):
        return lax.dot_general(turned, keys, contract_last, preferred_element_type=f32)

    token = lax.broadcasted_iota(jnp.int32, (rows, 1), 0) % TOKENS
    first = token < 2
    slot = lax.broadcasted_iota(jnp.int32, (rows, slots), 1)
    length = jnp.where(first, lengths[0], lengths[1])
    old = jnp.where(first, scores(k_old[0]), scores(k_old[1])) * score_scale
    old = jnp.where(slot < length, old, -1e30)
    fresh = scores(k_new[...]) * score_scale
    other = lax.broadcasted_iota(jnp.int32, fresh.shape, 1)
    keep = (other // 2 == token // 2) & (other <= token)
    fresh = jnp.where(keep, fresh, -1e30)
    highest = jnp.maximum(
        jnp.max(old, axis=1, keepdims=True), jnp.max(fresh, axis=1, keepdims=True)
    )
    old = jnp.exp(old - highest)
    fresh = jnp.exp(fresh - highest)
    denom = jnp.sum(old, axis=1, keepdims=True) + jnp.sum(fresh, axis=1, keepdims=True)
    mixed = (
        dot(jnp.where(first, old, 0.0).astype(bf16), v_old[0])
        + dot(jnp.where(first, 0.0, old).astype(bf16), v_old[1])
        + dot(fresh.astype(bf16), v_new[...])
    )
    out[...] = (mixed / denom).astype(bf16)


def attend(q, cosine, sine, cache_keys, cache_values, k_new, v_new, lengths):
    group_rows = q.shape[0] // KVH
    slots = cache_keys.shape[1]
    fresh_rows = k_new.shape[0]
    return pl.pallas_call(
        attention_kernel,
        out_shape=jax.ShapeDtypeStruct(q.shape, bf16),
        grid_spec=pltpu.PrefetchScalarGridSpec(
            num_scalar_prefetch=1,
            grid=(KVH,),
            in_specs=[
                pl.BlockSpec((group_rows, HD), lambda g, n: (g, 0)),
                pl.BlockSpec((group_rows, HD), lambda g, n: (0, 0)),
                pl.BlockSpec((group_rows, HD), lambda g, n: (0, 0)),
                pl.BlockSpec((2, slots, HD), lambda g, n: (0, 0, g)),
                pl.BlockSpec((2, slots, HD), lambda g, n: (0, 0, g)),
                pl.BlockSpec((fresh_rows, HD), lambda g, n: (0, g)),
                pl.BlockSpec((fresh_rows, HD), lambda g, n: (0, g)),
            ],
            out_specs=pl.BlockSpec((group_rows, HD), lambda g, n: (g, 0)),
        ),
        compiler_params=pltpu.CompilerParams(vmem_limit_bytes=24 * 1024 * 1024),
        cost_estimate=pl.CostEstimate(
            flops=8 * q.shape[0] * slots * HD,
            bytes_accessed=8 * slots * KVH * HD,
            transcendentals=q.shape[0] * slots,
        ),
        name="attention",
    )(lengths, q, cosine, sine, cache_keys, cache_values, k_new, v_new)


def z_ring(block):
    ahead, behind = [block], [block]
    for _ in range(NZ // 2):
        ahead.append(recv(ahead[-1], "z", 1))
    for _ in range(NZ // 2 - 1):
        behind.append(recv(behind[-1], "z", -1))
    return ahead + behind[:0:-1]


def gather_x_then_z(piece):
    line = jnp.stack([piece] + [recv(piece, "x", d) for d in (1, 2, 3)])
    return jnp.stack(z_ring(line), axis=1)


def gather_z_then_x(piece):
    line = jnp.stack(z_ring(piece))
    ahead, behind = recv(line, "x", 1), recv(line, "x", -1)
    cut = NZ // 2
    far = jnp.concatenate([recv(ahead[:cut], "x", 1), recv(behind[cut:], "x", -1)])
    return jnp.stack([line, ahead, far, behind])


def z_ring_sum(part):
    up = part(NZ // 2).astype(bf16)
    for j in range(NZ // 2 - 1, 0, -1):
        up = (part(j) + recv(up, "z", -1)).astype(bf16)
    down = part(NZ // 2 + 1).astype(bf16)
    for j in range(NZ // 2 + 2, NZ):
        down = (part(j) + recv(down, "z", 1)).astype(bf16)
    return part(0) + recv(up, "z", -1) + recv(down, "z", 1)


def scatter_z_then_x(part):
    line = z_ring_sum(part)
    out = line[0]
    for d in (1, 2, 3):
        out = out + recv(line[NX - d].astype(bf16), "x", d)
    return out


def scatter_x_then_z(part):
    far = part(2).astype(bf16)
    cut = NZ // 2
    ahead = part(1)
    ahead = jnp.concatenate([ahead[:cut] + recv(far[:cut], "x", -1), ahead[cut:]]).astype(bf16)
    behind = part(3)
    behind = jnp.concatenate([behind[:cut], behind[cut:] + recv(far[cut:], "x", 1)]).astype(bf16)
    line = part(0) + recv(ahead, "x", -1) + recv(behind, "x", 1)
    return z_ring_sum(lambda j: line[j])


def on_device(
    hidden, norm_gain, w_query, w_keyval, w_out, cache_keys, cache_values, cache_lengths, positions
):
    x, y, z, c = (lax.axis_index(a) for a in "xyzc")
    rows, steps, width = hidden.shape
    tokens = rows * steps
    half = width // 2
    quarter = half // 2
    head_cols = w_query.shape[1]
    keyval_cols = w_keyval.shape[2]

    def mine(array, axis):
        return lax.dynamic_slice_in_dim(array, c * half, half, axis)

    def others(array, axis):
        return lax.dynamic_slice_in_dim(array, (1 - c) * half, half, axis)

    w_query_mine = mine(w_query, 0)
    w_query_other = recv(others(w_query, 0), "c", 1)
    w_keyval_mine = jnp.concatenate(list(mine(w_keyval, 1)), axis=1)
    w_keyval_other = recv(jnp.concatenate(list(others(w_keyval, 1)), axis=1), "c", 1)
    w_out_mine = mine(w_out, 1)
    w_out_other = recv(others(w_out, 1), "c", 1)

    places = positions.astype(f32)[:, None] + jnp.arange(steps, dtype=f32)[None, :]
    angles = places.reshape(-1)[:, None] * rope_rates()
    cosine, sine = jnp.cos(angles), jnp.sin(angles)
    cosine = jnp.concatenate([cosine, cosine], axis=1)
    sine = jnp.concatenate([-sine, sine], axis=1)

    features = hidden.reshape(tokens, width).astype(f32)
    square_sums = lax.psum(jnp.sum(features * features, axis=-1), "y")
    inverse = lax.rsqrt(square_sums / (width * NY) + norm_epsilon)
    normed = (features * inverse[:, None] * norm_gain.astype(f32)).astype(bf16)

    own, swapped = mine(normed, 1), recv(others(normed, 1), "c", 1)
    piece = jnp.where(
        c == 0, jnp.concatenate([own, swapped]), jnp.concatenate([swapped, own])
    )
    gathered = [
        gather_x_then_z(piece[:, :quarter]).reshape(-1, quarter),
        gather_z_then_x(piece[:, quarter:]).reshape(-1, quarter),
    ]
    all_tokens = gathered[0].shape[0]
    block = all_tokens // NX

    def project(w_q, w_kv):
        q = sum(dot(g, w_q[i * quarter : (i + 1) * quarter]) for i, g in enumerate(gathered))
        kv = sum(
            lax.dot_general(
                w_kv[i * quarter : (i + 1) * quarter],
                g,
                (((0,), (1,)), ((), ())),
                preferred_element_type=f32,
            )
            for i, g in enumerate(gathered)
        )
        kv = kv.reshape(2 * keyval_cols, NX, block).transpose(1, 0, 2)
        return jnp.concatenate([q.reshape(NX, block, head_cols), kv], axis=1)

    partial = recv(project(w_query_other, w_keyval_other), "c", 1)
    partial = partial + project(w_query_mine, w_keyval_mine)

    def block_for(d):
        return lax.dynamic_index_in_dim(partial, (y + d - x + NX) % NX, 0, keepdims=False)

    summed = block_for(0)
    for d in (1, 2, 3):
        summed = summed + recv(block_for(d), "y", -d)
    summed = summed.astype(bf16)
    back = (NZ - z) % NZ
    q = roll_to(summed[:block].reshape(NZ, -1, head_cols), back)
    kv = roll_to(summed[block:].T.reshape(NZ, -1, 2 * keyval_cols), back)
    places_out = block // TOKENS
    q = q.reshape(places_out, TOKENS, head_cols // HD, HD).transpose(0, 2, 1, 3)
    q = q.reshape(places_out, -1, HD)
    kv = kv.reshape(places_out, 1, -1)
    arrived = lax.all_to_all(
        jnp.concatenate([q, kv], axis=1), ("x", "z", "c"), split_axis=0, concat_axis=0, tiled=True
    )
    q_rows = q.shape[1]
    queries = arrived[:, :q_rows].reshape(-1, HD)
    keyvals = arrived[:, q_rows].reshape(places_out, TOKENS, 2, keyval_cols)
    keyvals = keyvals.transpose(2, 1, 0, 3).reshape(2, TOKENS, KVH, HD)
    fresh_keys = keyvals[0].astype(f32)
    turned_keys = (
        fresh_keys * cosine[:, None] + jnp.roll(fresh_keys, HALF, axis=-1) * sine[:, None]
    ).astype(bf16)
    new = jnp.stack([turned_keys, keyvals[1]]).reshape(2, TOKENS, KVH * HD)
    padded = jnp.pad(new, ((0, 0), (0, 16 - TOKENS), (0, 0)))
    group = HQ // KVH
    attended = attend(
        queries,
        jnp.tile(cosine, (group, 1)),
        jnp.tile(sine, (group, 1)),
        cache_keys,
        cache_values,
        padded[0],
        padded[1],
        cache_lengths,
    )
    returned = lax.all_to_all(
        attended.reshape(places_out, -1, HD), ("x", "z", "c"), split_axis=0, concat_axis=0, tiled=True
    )
    returned = returned.reshape(places_out, head_cols // HD, TOKENS, HD).transpose(0, 2, 1, 3)
    returned = roll_to(returned.reshape(NZ, -1, head_cols), z)
    line = jnp.stack([returned] + [recv(returned, "y", d) for d in (1, 2, 3)])
    left_own = roll_to(line, (x - y + NX) % NX)
    left_other = recv(left_own, "c", 1)

    def out_part(pick, columns):
        a, b = pick(left_own), pick(left_other)
        product = dot(a.reshape(-1, head_cols), w_out_mine[:, columns])
        product = product + dot(b.reshape(-1, head_cols), w_out_other[:, columns])
        return product.reshape(a.shape[:-1] + (quarter,))

    branch = jnp.concatenate(
        [
            scatter_z_then_x(lambda j: out_part(lambda a: a[:, j], slice(0, quarter))),
            scatter_x_then_z(lambda i: out_part(lambda a: a[i], slice(quarter, half))),
        ],
        axis=1,
    ).astype(bf16)
    kept = lax.dynamic_slice_in_dim(branch, c * tokens, tokens, 0)
    got = recv(lax.dynamic_slice_in_dim(branch, (1 - c) * tokens, tokens, 0), "c", 1)
    branch = jnp.where(
        c == 0, jnp.concatenate([kept, got], axis=1), jnp.concatenate([got, kept], axis=1)
    )
    return (
        branch.reshape(rows, steps, width),
        new.reshape(2, TOKENS // steps, steps, KVH * HD),
    )


def solution(mesh):
    fine = Mesh(mesh.devices.reshape(NY, NX, NZ, NC), ("y", "x", "z", "c"))
    gy = ("x", "z", "c")
    everywhere = ("y", "x", "z", "c")
    return jax.shard_map(
        on_device,
        mesh=fine,
        in_specs=(
            P(gy, None, "y"),
            P("y"),
            P("y", gy),
            P(None, "y", gy),
            P(gy, "y"),
            P(everywhere, None, None),
            P(everywhere, None, None),
            P(everywhere),
            P(everywhere),
        ),
        out_specs=(P(gy, None, "y"), P(None, everywhere, None, None)),
        check_vma=False,
    )
```

```python
import math

import jax
import jax.numpy as jnp
from jax import lax
from jax.experimental import pallas as pl
from jax.experimental.pallas import tpu as pltpu
from jax.sharding import Mesh
from jax.sharding import PartitionSpec as P

HQ = 128
KVH = 8
HD = 128
HALF = HD // 2
TOKENS = 4
NX, NY, NZ, NC = 4, 4, 8, 2
f32 = jnp.float32
bf16 = jnp.bfloat16

norm_epsilon = 1e-05


def rope_rates():
    index = jnp.arange(HD // 2, dtype=jnp.float32)
    rates = 1.0 / jnp.power(500000.0, 2.0 * index / HD)
    wavelength = 2.0 * math.pi / rates
    smooth = (8192.0 / wavelength - 1.0) / 3.0
    blended = (1.0 - smooth) * rates / 8.0 + smooth * rates
    return jnp.where(
        wavelength > 8192.0, rates / 8.0, jnp.where(wavelength < 2048.0, rates, blended)
    )


def recv(block, axis, distance):
    size = lax.axis_size(axis)
    return lax.ppermute(block, axis, [((i + distance) % size, i) for i in range(size)])


def roll_to(blocks, start):
    return lax.dynamic_slice_in_dim(
        jnp.concatenate([blocks, blocks], axis=0), start, blocks.shape[0], 0
    )


def dot(a, b):
    return jnp.dot(a, b, preferred_element_type=f32)


def attention_kernel(lengths, q, cosine, sine, k_old, v_old, k_new, v_new, out):
    queries = q[...].astype(f32)
    turned = (queries * cosine[...] + pltpu.roll(queries, HALF, 1) * sine[...]).astype(bf16)
    rows = turned.shape[0]
    slots = k_old.shape[1]
    contract_last = (((1,), (1,)), ((), ()))
    score_scale = HD ** (-0.5)

    def scores(keys):
        return lax.dot_general(turned, keys, contract_last, preferred_element_type=f32)

    token = lax.broadcasted_iota(jnp.int32, (rows, 1), 0) % TOKENS
    first = token < 2
    slot = lax.broadcasted_iota(jnp.int32, (rows, slots), 1)
    length = jnp.where(first, lengths[0], lengths[1])
    old = jnp.where(first, scores(k_old[0]), scores(k_old[1])) * score_scale
    old = jnp.where(slot < length, old, -1e30)
    fresh = scores(k_new[...]) * score_scale
    other = lax.broadcasted_iota(jnp.int32, fresh.shape, 1)
    keep = (other // 2 == token // 2) & (other <= token)
    fresh = jnp.where(keep, fresh, -1e30)
    highest = jnp.maximum(
        jnp.max(old, axis=1, keepdims=True), jnp.max(fresh, axis=1, keepdims=True)
    )
    old = jnp.exp(old - highest)
    fresh = jnp.exp(fresh - highest)
    denom = jnp.sum(old, axis=1, keepdims=True) + jnp.sum(fresh, axis=1, keepdims=True)
    mixed = (
        dot(jnp.where(first, old, 0.0).astype(bf16), v_old[0])
        + dot(jnp.where(first, 0.0, old).astype(bf16), v_old[1])
        + dot(fresh.astype(bf16), v_new[...])
    )
    out[...] = (mixed / denom).astype(bf16)


def attend(q, cosine, sine, cache_keys, cache_values, k_new, v_new, lengths):
    group_rows = q.shape[0] // KVH
    slots = cache_keys.shape[1]
    fresh_rows = k_new.shape[0]
    return pl.pallas_call(
        attention_kernel,
        out_shape=jax.ShapeDtypeStruct(q.shape, bf16),
        grid_spec=pltpu.PrefetchScalarGridSpec(
            num_scalar_prefetch=1,
            grid=(KVH,),
            in_specs=[
                pl.BlockSpec((group_rows, HD), lambda g, n: (g, 0)),
                pl.BlockSpec((group_rows, HD), lambda g, n: (0, 0)),
                pl.BlockSpec((group_rows, HD), lambda g, n: (0, 0)),
                pl.BlockSpec((2, slots, HD), lambda g, n: (0, 0, g)),
                pl.BlockSpec((2, slots, HD), lambda g, n: (0, 0, g)),
                pl.BlockSpec((fresh_rows, HD), lambda g, n: (0, g)),
                pl.BlockSpec((fresh_rows, HD), lambda g, n: (0, g)),
            ],
            out_specs=pl.BlockSpec((group_rows, HD), lambda g, n: (g, 0)),
        ),
        compiler_params=pltpu.CompilerParams(vmem_limit_bytes=56 * 1024 * 1024),
        cost_estimate=pl.CostEstimate(
            flops=8 * q.shape[0] * slots * HD,
            bytes_accessed=8 * slots * KVH * HD,
            transcendentals=q.shape[0] * slots,
        ),
        name="attention",
    )(lengths, q, cosine, sine, cache_keys, cache_values, k_new, v_new)


def gather_rows(piece):
    middle = NZ // 2
    own_up, own_down = [piece[None]], [piece[None]]
    rest = jnp.stack([recv(piece, "x", d) for d in (1, 2, 3)])
    rest_up, rest_down = [rest], [rest]
    for k in range(1, middle):
        if k > 2:
            own_up[-1], own_down[-1], _, _ = lax.optimization_barrier(
                (own_up[-1], own_down[-1], rest_up[-2], rest_down[-2])
            )
        own_up.append(recv(own_up[-1], "z", 1))
        own_down.append(recv(own_down[-1], "z", -1))
        rest_up.append(recv(rest_up[-1], "z", 1))
        rest_down.append(recv(rest_down[-1], "z", -1))
    own = own_up + [recv(own_down[-1], "z", -1)] + own_down[:0:-1]
    far = [recv(rest_up[-1][:2], "z", 1), recv(rest_down[-1][2:], "z", -1)]
    rest = rest_up + [jnp.concatenate(far)] + rest_down[:0:-1]
    own, rest = jnp.stack(own), jnp.stack(rest, axis=1)
    return jnp.concatenate([own.reshape((1,) + rest.shape[1:]), rest])


def z_ring_sum(part, cut):
    middle = NZ // 2
    far = part(middle).astype(bf16)
    up, down = far[:cut], far[cut:]
    for j in range(1, middle):
        above, below = part(middle - j), part(middle + j)
        if up.shape[0]:
            got = recv(up, "z", -1)
            above = jnp.concatenate([above[: got.shape[0]] + got, above[got.shape[0] :]])
        if down.shape[0]:
            got = recv(down, "z", 1)
            left = below.shape[0] - got.shape[0]
            below = jnp.concatenate([below[:left], below[left:] + got])
        up, down = above.astype(bf16), below.astype(bf16)
    return part(0) + recv(up, "z", -1) + recv(down, "z", 1)


def scatter_rows(part_own, part_rest):
    rest = z_ring_sum(part_rest, 2)
    out = z_ring_sum(part_own, 0)[0]
    for d in (1, 2, 3):
        out = out + recv(rest[NX - d - 1].astype(bf16), "x", d)
    return out


def on_device(
    hidden, norm_gain, w_query, w_keyval, w_out, cache_keys, cache_values, cache_lengths, positions
):
    x, y, z, c = (lax.axis_index(a) for a in "xyzc")
    rows, steps, width = hidden.shape
    tokens = rows * steps
    half = width // 2
    head_cols = w_query.shape[1]
    keyval_cols = w_keyval.shape[2]

    def mine(array, axis):
        return lax.dynamic_slice_in_dim(array, c * half, half, axis)

    def others(array, axis):
        return lax.dynamic_slice_in_dim(array, (1 - c) * half, half, axis)

    w_query_mine = mine(w_query, 0)
    w_query_other = recv(others(w_query, 0), "c", 1)
    w_keyval_mine = jnp.concatenate(list(mine(w_keyval, 1)), axis=1)
    w_keyval_other = recv(jnp.concatenate(list(others(w_keyval, 1)), axis=1), "c", 1)
    w_out_mine = mine(w_out, 1)
    w_out_other = recv(others(w_out, 1), "c", 1)

    places = positions.astype(f32)[:, None] + jnp.arange(steps, dtype=f32)[None, :]
    angles = places.reshape(-1)[:, None] * rope_rates()
    cosine, sine = jnp.cos(angles), jnp.sin(angles)
    cosine = jnp.concatenate([cosine, cosine], axis=1)
    sine = jnp.concatenate([-sine, sine], axis=1)

    features = hidden.reshape(tokens, width).astype(f32)
    square_sums = lax.psum(jnp.sum(features * features, axis=-1), "y")
    inverse = lax.rsqrt(square_sums / (width * NY) + norm_epsilon)
    normed = (features * inverse[:, None] * norm_gain.astype(f32)).astype(bf16)

    own, swapped = mine(normed, 1), recv(others(normed, 1), "c", 1)
    piece = jnp.where(
        c == 0, jnp.concatenate([own, swapped]), jnp.concatenate([swapped, own])
    )
    gathered = gather_rows(piece).reshape(-1, half)
    block = gathered.shape[0] // NX

    def project(w_q, w_kv):
        kv = lax.dot_general(
            w_kv, gathered, (((0,), (1,)), ((), ())), preferred_element_type=f32
        )
        kv = kv.reshape(2 * keyval_cols, NX, block).transpose(1, 0, 2)
        return jnp.concatenate([dot(gathered, w_q).reshape(NX, block, head_cols), kv], axis=1)

    partial = recv(project(w_query_other, w_keyval_other), "c", 1)
    partial = partial + project(w_query_mine, w_keyval_mine)

    def block_for(d):
        return lax.dynamic_index_in_dim(partial, (y + d - x + NX) % NX, 0, keepdims=False)

    summed = block_for(0)
    for d in (1, 2, 3):
        summed = summed + recv(block_for(d), "y", -d)
    summed = summed.astype(bf16)
    back = (NZ - z) % NZ
    q = roll_to(summed[:block].reshape(NZ, -1, head_cols), back)
    kv = roll_to(summed[block:].T.reshape(NZ, -1, 2 * keyval_cols), back)
    places_out = block // TOKENS
    q = q.reshape(places_out, TOKENS, head_cols // HD, HD).transpose(0, 2, 1, 3)
    q = q.reshape(places_out, -1, HD)
    kv = kv.reshape(places_out, 1, -1)
    arrived = lax.all_to_all(
        jnp.concatenate([q, kv], axis=1), ("x", "z", "c"), split_axis=0, concat_axis=0, tiled=True
    )
    q_rows = q.shape[1]
    queries = arrived[:, :q_rows].reshape(-1, HD)
    keyvals = arrived[:, q_rows].reshape(places_out, TOKENS, 2, keyval_cols)
    keyvals = keyvals.transpose(2, 1, 0, 3).reshape(2, TOKENS, KVH, HD)
    fresh_keys = keyvals[0].astype(f32)
    turned_keys = (
        fresh_keys * cosine[:, None] + jnp.roll(fresh_keys, HALF, axis=-1) * sine[:, None]
    ).astype(bf16)
    new = jnp.stack([turned_keys, keyvals[1]]).reshape(2, TOKENS, KVH * HD)
    padded = jnp.pad(new, ((0, 0), (0, 16 - TOKENS), (0, 0)))
    group = HQ // KVH
    attended = attend(
        queries,
        jnp.tile(cosine, (group, 1)),
        jnp.tile(sine, (group, 1)),
        cache_keys,
        cache_values,
        padded[0],
        padded[1],
        cache_lengths,
    )
    returned = lax.all_to_all(
        attended.reshape(places_out, -1, HD), ("x", "z", "c"), split_axis=0, concat_axis=0, tiled=True
    )
    returned = returned.reshape(places_out, head_cols // HD, TOKENS, HD).transpose(0, 2, 1, 3)
    returned = roll_to(returned.reshape(NZ, -1, head_cols), z)
    line = jnp.stack([returned] + [recv(returned, "y", d) for d in (1, 2, 3)])

    def by_distance(blocks):
        at = [
            lax.dynamic_index_in_dim(blocks, (x + i - y + NX) % NX, 0, keepdims=False)
            for i in range(NX)
        ]
        return at[0][:, None], jnp.stack(at[1:], axis=1)

    own_mine, rest_mine = by_distance(line)
    own_other, rest_other = by_distance(recv(line, "c", 1))

    def out_part(a, b):
        def part(j):
            product = dot(a[j].reshape(-1, head_cols), w_out_mine)
            product = product + dot(b[j].reshape(-1, head_cols), w_out_other)
            return product.reshape(a.shape[1:-1] + (half,))

        return part

    branch = scatter_rows(out_part(own_mine, own_other), out_part(rest_mine, rest_other))
    branch = branch.astype(bf16)
    kept = lax.dynamic_slice_in_dim(branch, c * tokens, tokens, 0)
    got = recv(lax.dynamic_slice_in_dim(branch, (1 - c) * tokens, tokens, 0), "c", 1)
    branch = jnp.where(
        c == 0, jnp.concatenate([kept, got], axis=1), jnp.concatenate([got, kept], axis=1)
    )
    return (
        branch.reshape(rows, steps, width),
        new.reshape(2, TOKENS // steps, steps, KVH * HD),
    )


def solution(mesh):
    fine = Mesh(mesh.devices.reshape(NY, NX, NZ, NC), ("y", "x", "z", "c"))
    gy = ("x", "z", "c")
    everywhere = ("y", "x", "z", "c")
    return jax.shard_map(
        on_device,
        mesh=fine,
        in_specs=(
            P(gy, None, "y"),
            P("y"),
            P("y", gy),
            P(None, "y", gy),
            P(gy, "y"),
            P(everywhere, None, None),
            P(everywhere, None, None),
            P(everywhere),
            P(everywhere),
        ),
        out_specs=(P(gy, None, "y"), P(None, everywhere, None, None)),
        check_vma=False,
    )
```

```python
import math

import jax
import jax.numpy as jnp
from jax import lax
from jax.experimental import pallas as pl
from jax.experimental.pallas import tpu as pltpu
from jax.sharding import Mesh
from jax.sharding import PartitionSpec as P

HQ = 128
KVH = 8
HD = 128
HALF = HD // 2
TOKENS = 4
NX, NY, NZ, NC = 4, 4, 8, 2
f32 = jnp.float32
bf16 = jnp.bfloat16

norm_epsilon = 1e-05


def rope_rates():
    index = jnp.arange(HD // 2, dtype=jnp.float32)
    rates = 1.0 / jnp.power(500000.0, 2.0 * index / HD)
    wavelength = 2.0 * math.pi / rates
    smooth = (8192.0 / wavelength - 1.0) / 3.0
    blended = (1.0 - smooth) * rates / 8.0 + smooth * rates
    return jnp.where(
        wavelength > 8192.0, rates / 8.0, jnp.where(wavelength < 2048.0, rates, blended)
    )


def recv(block, axis, distance):
    size = lax.axis_size(axis)
    return lax.ppermute(block, axis, [((i + distance) % size, i) for i in range(size)])


def roll_to(blocks, start):
    return lax.dynamic_slice_in_dim(
        jnp.concatenate([blocks, blocks], axis=0), start, blocks.shape[0], 0
    )


def dot(a, b):
    return jnp.dot(a, b, preferred_element_type=f32)


HEADS_AT_ONCE = 2


def attention_kernel(lengths, q, cosine, sine, k_old, v_old, k_new, v_new, out):
    rows = q.shape[0] // HEADS_AT_ONCE
    slots = k_old.shape[1]
    repeats = rows // cosine.shape[0]
    cosines = jnp.concatenate([cosine[...]] * repeats)
    sines = jnp.concatenate([sine[...]] * repeats)
    contract_last = (((1,), (1,)), ((), ()))
    score_scale = HD ** (-0.5)
    token = lax.broadcasted_iota(jnp.int32, (rows, 1), 0) % TOKENS
    first = token < 2
    slot = lax.broadcasted_iota(jnp.int32, (rows, slots), 1)
    valid = slot < jnp.where(first, lengths[0], lengths[1])
    for head in range(HEADS_AT_ONCE):
        mine = slice(head * rows, (head + 1) * rows)
        lanes = slice(head * HD, (head + 1) * HD)
        queries = q[mine, :].astype(f32)
        turned = (queries * cosines + pltpu.roll(queries, HALF, 1) * sines).astype(bf16)

        def scores(keys):
            return lax.dot_general(turned, keys, contract_last, preferred_element_type=f32)

        old = jnp.where(first, scores(k_old[0, :, lanes]), scores(k_old[1, :, lanes]))
        old = jnp.where(valid, old * score_scale, -1e30)
        fresh = scores(k_new[:, lanes]) * score_scale
        other = lax.broadcasted_iota(jnp.int32, fresh.shape, 1)
        keep = (other // 2 == token // 2) & (other <= token)
        fresh = jnp.where(keep, fresh, -1e30)
        highest = jnp.maximum(
            jnp.max(old, axis=1, keepdims=True), jnp.max(fresh, axis=1, keepdims=True)
        )
        old = jnp.exp(old - highest)
        fresh = jnp.exp(fresh - highest)
        denom = jnp.sum(old, axis=1, keepdims=True) + jnp.sum(fresh, axis=1, keepdims=True)
        mixed = (
            dot(jnp.where(first, old, 0.0).astype(bf16), v_old[0, :, lanes])
            + dot(jnp.where(first, 0.0, old).astype(bf16), v_old[1, :, lanes])
            + dot(fresh.astype(bf16), v_new[:, lanes])
        )
        out[mine, :] = (mixed / denom).astype(bf16)


def attend(q, cosine, sine, cache_keys, cache_values, k_new, v_new, lengths):
    step_rows = q.shape[0] // KVH * HEADS_AT_ONCE
    step_cols = HD * HEADS_AT_ONCE
    slots = cache_keys.shape[1]
    fresh_rows = k_new.shape[0]
    return pl.pallas_call(
        attention_kernel,
        out_shape=jax.ShapeDtypeStruct(q.shape, bf16),
        grid_spec=pltpu.PrefetchScalarGridSpec(
            num_scalar_prefetch=1,
            grid=(KVH // HEADS_AT_ONCE,),
            in_specs=[
                pl.BlockSpec((step_rows, HD), lambda g, n: (g, 0)),
                pl.BlockSpec(cosine.shape, lambda g, n: (0, 0)),
                pl.BlockSpec(sine.shape, lambda g, n: (0, 0)),
                pl.BlockSpec((2, slots, step_cols), lambda g, n: (0, 0, g)),
                pl.BlockSpec((2, slots, step_cols), lambda g, n: (0, 0, g)),
                pl.BlockSpec((fresh_rows, step_cols), lambda g, n: (0, g)),
                pl.BlockSpec((fresh_rows, step_cols), lambda g, n: (0, g)),
            ],
            out_specs=pl.BlockSpec((step_rows, HD), lambda g, n: (g, 0)),
        ),
        compiler_params=pltpu.CompilerParams(vmem_limit_bytes=56 * 1024 * 1024),
        cost_estimate=pl.CostEstimate(
            flops=8 * q.shape[0] * slots * HD,
            bytes_accessed=8 * slots * KVH * HD,
            transcendentals=q.shape[0] * slots,
        ),
        name="attention",
    )(lengths, q, cosine, sine, cache_keys, cache_values, k_new, v_new)


FIRST, SECOND = 0, 1
DIRECTIONS = {"z+": ("z", 1), "z-": ("z", -1), "x+": ("x", 1), "x-": ("x", -1)}


def tree_rounds():
    a, b = FIRST, SECOND
    return [
        {
            "z+": [(b, 0, 1), (a, 0, 1)],
            "z-": [(b, 0, 7), (a, 0, 7)],
            "x+": [(a, 1, 0), (b, 1, 0)],
            "x-": [(a, 3, 0), (b, 3, 0)],
        },
        {
            "z+": [(b, 0, 2), (a, 0, 2), (a, 1, 1), (a, 3, 1)],
            "z-": [(b, 0, 6), (a, 0, 6), (a, 1, 7), (a, 3, 7)],
            "x+": [(a, 2, 0), (b, 1, 1), (b, 1, 7)],
            "x-": [(b, 2, 0), (b, 3, 1), (b, 3, 7)],
        },
        {
            "z+": [(b, 0, 3), (a, 0, 3), (a, 1, 2), (a, 3, 2), (a, 2, 1)],
            "z-": [(b, 0, 5), (a, 0, 5), (a, 1, 6), (a, 3, 6), (a, 2, 7)],
            "x+": [(b, 2, 1), (b, 1, 2), (b, 1, 6)],
            "x-": [(b, 2, 7), (b, 3, 2), (b, 3, 6)],
        },
        {
            "z+": [(a, 0, 4), (a, 1, 3), (a, 3, 3), (a, 2, 2)],
            "z-": [(b, 0, 4), (a, 1, 5), (a, 3, 5), (a, 2, 6)],
            "x+": [(b, 2, 2), (b, 1, 3), (b, 1, 5)],
            "x-": [(b, 2, 6), (b, 3, 3), (b, 3, 5)],
        },
        {
            "z+": [(a, 1, 4), (a, 2, 3)],
            "z-": [(a, 3, 4), (a, 2, 5)],
            "x+": [(b, 2, 3), (b, 1, 4)],
            "x-": [(b, 2, 5), (b, 3, 4)],
        },
        {"z+": [(a, 2, 4)], "x-": [(b, 2, 4)]},
    ]


def seen_from(item, direction):
    which, dx, dz = item
    axis, sign = DIRECTIONS[direction]
    return (which, (dx - sign) % NX, dz) if axis == "x" else (which, dx, (dz - sign) % NZ)


def gather_rows(piece):
    rows = piece.shape[0] // 2
    messages = [piece]
    places = {(FIRST, 0, 0): (0, 0), (SECOND, 0, 0): (0, rows)}
    for exchange in tree_rounds():
        got = []
        for direction, items in exchange.items():
            held = [places[seen_from(item, direction)] for item in items]
            runs = []
            for message, row in held:
                if runs and runs[-1][0] == message and runs[-1][2] == row:
                    runs[-1][2] += rows
                else:
                    runs.append([message, row, row + rows])
            parts = [messages[m][lo:hi] for m, lo, hi in runs]
            got.append((recv(jnp.concatenate(parts), *DIRECTIONS[direction]), items))
        for message, items in got:
            for k, item in enumerate(items):
                places[item] = (len(messages), k * rows)
            messages.append(message)
    return messages, places


def scatter_rows(terms):
    total = dict(terms)
    for exchange in reversed(tree_rounds()):
        got = []
        for direction, items in exchange.items():
            axis, sign = DIRECTIONS[direction]
            message = jnp.concatenate([total[item] for item in items]).astype(bf16)
            got.append((recv(message, axis, -sign), direction, items))
        arrived = lax.optimization_barrier([message for message, _, _ in got])
        for message, (_, direction, items) in zip(arrived, got):
            rows = message.shape[0] // len(items)
            for k, item in enumerate(items):
                target = seen_from(item, direction)
                total[target] = total[target] + message[k * rows : (k + 1) * rows]
    return total[(FIRST, 0, 0)], total[(SECOND, 0, 0)]


def project(messages, places, w_mine, w_other, w_keyval):
    rows, width = messages[0].shape[0] // 2, messages[0].shape[1]
    block = 2 * rows * NZ
    columns = w_mine.shape[1]
    fresh = w_keyval.shape[0] // 2
    count = len(messages)

    def kernel(*refs):
        sources, (mine, other, keyval, out_mine, out_other, held) = refs[:count], refs[count:]
        for dx in range(NX):
            for dz in range(NZ):
                for which in (FIRST, SECOND):
                    message, row = places[(which, dx, dz)]
                    to = dx * block + (dz * 2 + which) * rows
                    held[to : to + rows, :] = sources[message][row : row + rows, :]

        @pl.loop(0, NX)
        def _(dx):
            features = held[pl.ds(pl.multiple_of(dx * block, block), block), :]
            out_mine[dx, :block, :] = dot(features, mine[...])
            out_other[dx, :block, :] = dot(features, other[...])
            kv = lax.dot_general(
                keyval[...], features, (((1,), (1,)), ((), ())), preferred_element_type=f32
            )
            out_mine[dx, block:, :] = kv[:fresh]
            out_other[dx, block:, :] = kv[fresh:]

    shape = jax.ShapeDtypeStruct((NX, block + fresh, columns), f32)
    spec = pl.BlockSpec(memory_space=pltpu.VMEM)
    return pl.pallas_call(
        kernel,
        out_shape=[shape, shape],
        in_specs=[spec] * (count + 3),
        out_specs=[spec, spec],
        scratch_shapes=[pltpu.VMEM((NX * block, width), bf16)],
        compiler_params=pltpu.CompilerParams(vmem_limit_bytes=32 * 1024 * 1024),
        cost_estimate=pl.CostEstimate(
            flops=2 * NX * block * width * (2 * columns + 2 * fresh),
            bytes_accessed=2 * NX * block * width + 8 * NX * block * columns,
            transcendentals=0,
        ),
        name="project",
    )(*messages, w_mine, w_other, w_keyval)


def on_device(
    hidden, norm_gain, w_query, w_keyval, w_out, cache_keys, cache_values, cache_lengths, positions
):
    x, y, z, c = (lax.axis_index(a) for a in "xyzc")
    rows, steps, width = hidden.shape
    tokens = rows * steps
    half = width // 2
    head_cols = w_query.shape[1]
    keyval_cols = w_keyval.shape[2]

    def mine(array, axis):
        return lax.dynamic_slice_in_dim(array, c * half, half, axis)

    def others(array, axis):
        return lax.dynamic_slice_in_dim(array, (1 - c) * half, half, axis)

    def in_core_order(own, swapped, axis=0):
        return jnp.where(
            c == 0,
            jnp.concatenate([own, swapped], axis=axis),
            jnp.concatenate([swapped, own], axis=axis),
        )

    raw = hidden.reshape(tokens, width)
    swapped = recv(others(raw, 1), "c", 1)
    features = raw.astype(f32)
    squares = jnp.sum(features * features, axis=-1)
    nothing = jnp.zeros_like(squares)
    square_sums = lax.psum(in_core_order(squares, nothing), ("y", "c"))
    inverse = lax.rsqrt(square_sums / (width * NY) + norm_epsilon)
    features = in_core_order(mine(raw, 1), swapped).astype(f32)
    gain = mine(norm_gain, 0).astype(f32)
    piece = (features * inverse[:, None] * gain).astype(bf16)
    messages, item_places = gather_rows(piece)

    w_query, w_keyval, w_out, _ = lax.optimization_barrier(
        (w_query, w_keyval, w_out, messages[1])
    )
    w_query_mine = mine(w_query, 0)
    w_query_other = recv(others(w_query, 0), "c", 1)
    w_keyval = w_keyval.transpose(0, 2, 1).reshape(2 * keyval_cols, width)
    w_keyval = jnp.concatenate([mine(w_keyval, 1), recv(others(w_keyval, 1), "c", 1)])
    w_out_mine = mine(w_out, 1)
    w_out_other = recv(others(w_out, 1), "c", 1)

    places = positions.astype(f32)[:, None] + jnp.arange(steps, dtype=f32)[None, :]
    angles = places.reshape(-1)[:, None] * rope_rates()
    cosine, sine = jnp.cos(angles), jnp.sin(angles)
    cosine = jnp.concatenate([cosine, cosine], axis=1)
    sine = jnp.concatenate([-sine, sine], axis=1)

    partial, partial_other = project(
        messages, item_places, w_query_mine, w_query_other, w_keyval
    )
    partial = partial + recv(partial_other, "c", 1)
    block = partial.shape[1] - 2 * keyval_cols

    def block_for(d):
        return lax.dynamic_index_in_dim(partial, (y + d - x + NX) % NX, 0, keepdims=False)

    summed = block_for(0)
    for d in (1, 2, 3):
        summed = summed + recv(block_for(d), "y", -d)
    summed = summed.astype(bf16)
    back = (NZ - z) % NZ
    q = roll_to(summed[:block].reshape(NZ, -1, head_cols), back)
    kv = roll_to(summed[block:].T.reshape(NZ, -1, 2 * keyval_cols), back)
    places_out = block // TOKENS
    q = q.reshape(places_out, TOKENS, head_cols // HD, HD).transpose(0, 2, 1, 3)
    q = q.reshape(places_out, -1, HD)
    kv = kv.reshape(places_out, 1, -1)
    arrived = lax.all_to_all(
        jnp.concatenate([q, kv], axis=1), ("x", "z", "c"), split_axis=0, concat_axis=0, tiled=True
    )
    q_rows = q.shape[1]
    queries = arrived[:, :q_rows].reshape(-1, HD)
    keyvals = arrived[:, q_rows].reshape(places_out, TOKENS, 2, keyval_cols)
    keyvals = keyvals.transpose(2, 1, 0, 3).reshape(2, TOKENS, KVH, HD)
    fresh_keys = keyvals[0].astype(f32)
    turned_keys = (
        fresh_keys * cosine[:, None] + jnp.roll(fresh_keys, HALF, axis=-1) * sine[:, None]
    ).astype(bf16)
    new = jnp.stack([turned_keys, keyvals[1]]).reshape(2, TOKENS, KVH * HD)
    padded = jnp.pad(new, ((0, 0), (0, 16 - TOKENS), (0, 0)))
    attended = attend(
        queries,
        jnp.tile(cosine, (2, 1)),
        jnp.tile(sine, (2, 1)),
        cache_keys,
        cache_values,
        padded[0],
        padded[1],
        cache_lengths,
    )
    returned = lax.all_to_all(
        attended.reshape(places_out, -1, HD), ("x", "z", "c"), split_axis=0, concat_axis=0, tiled=True
    )
    returned = returned.reshape(places_out, head_cols // HD, TOKENS, HD).transpose(0, 2, 1, 3)
    returned = roll_to(returned.reshape(NZ, -1, head_cols), z)
    line = jnp.stack([returned] + [recv(returned, "y", d) for d in (1, 2, 3)])

    left = jnp.concatenate(
        [lax.dynamic_index_in_dim(line, (x + i - y + NX) % NX, 0) for i in range(NX)]
    ).reshape(NX, block, head_cols)
    left_other = recv(left, "c", 1)
    terms = {}
    for dx in (2, 1, 3, 0):
        product = dot(left[dx], w_out_mine) + dot(left_other[dx], w_out_other)
        product = product.reshape(NZ, 2, tokens, half)
        for dz in range(NZ):
            for which in (FIRST, SECOND):
                terms[(which, dx, dz)] = product[dz, which]
    branch = scatter_rows(terms)
    kept = jnp.where(c == 0, branch[0], branch[1]).astype(bf16)
    got = recv(jnp.where(c == 0, branch[1], branch[0]).astype(bf16), "c", 1)
    branch = in_core_order(kept, got, axis=1)
    return (
        branch.reshape(rows, steps, width),
        new.reshape(2, TOKENS // steps, steps, KVH * HD),
    )


def solution(mesh):
    fine = Mesh(mesh.devices.reshape(NY, NX, NZ, NC), ("y", "x", "z", "c"))
    gy = ("x", "z", "c")
    everywhere = ("y", "x", "z", "c")
    return jax.shard_map(
        on_device,
        mesh=fine,
        in_specs=(
            P(gy, None, "y"),
            P("y"),
            P("y", gy),
            P(None, "y", gy),
            P(gy, "y"),
            P(everywhere, None, None),
            P(everywhere, None, None),
            P(everywhere),
            P(everywhere),
        ),
        out_specs=(P(gy, None, "y"), P(None, everywhere, None, None)),
        check_vma=False,
    )
```

```python
import math

import jax
import jax.numpy as jnp
from jax import lax
from jax.experimental import pallas as pl
from jax.experimental.pallas import tpu as pltpu
from jax.sharding import Mesh
from jax.sharding import PartitionSpec as P

HQ = 128
KVH = 8
HD = 128
HALF = HD // 2
TOKENS = 4
NX, NY, NZ, NC = 4, 4, 8, 2
f32 = jnp.float32
bf16 = jnp.bfloat16

norm_epsilon = 1e-05


def rope_rates():
    index = jnp.arange(HD // 2, dtype=jnp.float32)
    rates = 1.0 / jnp.power(500000.0, 2.0 * index / HD)
    wavelength = 2.0 * math.pi / rates
    smooth = (8192.0 / wavelength - 1.0) / 3.0
    blended = (1.0 - smooth) * rates / 8.0 + smooth * rates
    return jnp.where(
        wavelength > 8192.0, rates / 8.0, jnp.where(wavelength < 2048.0, rates, blended)
    )


def recv(block, axis, distance):
    size = lax.axis_size(axis)
    return lax.ppermute(block, axis, [((i + distance) % size, i) for i in range(size)])


def roll_to(blocks, start):
    return lax.dynamic_slice_in_dim(
        jnp.concatenate([blocks, blocks], axis=0), start, blocks.shape[0], 0
    )


def dot(a, b):
    return jnp.dot(a, b, preferred_element_type=f32)


HEADS_AT_ONCE = 2


def attention_kernel(lengths, q, cosine, sine, k_old, v_old, k_new, v_new, out):
    rows = q.shape[0] // HEADS_AT_ONCE
    slots = k_old.shape[1]
    repeats = rows // cosine.shape[0]
    cosines = jnp.concatenate([cosine[...]] * repeats)
    sines = jnp.concatenate([sine[...]] * repeats)
    contract_last = (((1,), (1,)), ((), ()))
    score_scale = HD ** (-0.5)
    token = lax.broadcasted_iota(jnp.int32, (rows, 1), 0) % TOKENS
    first = token < 2
    slot = lax.broadcasted_iota(jnp.int32, (rows, slots), 1)
    valid = slot < jnp.where(first, lengths[0], lengths[1])
    for head in range(HEADS_AT_ONCE):
        mine = slice(head * rows, (head + 1) * rows)
        lanes = slice(head * HD, (head + 1) * HD)
        queries = q[mine, :].astype(f32)
        turned = (queries * cosines + pltpu.roll(queries, HALF, 1) * sines).astype(bf16)

        def scores(keys):
            return lax.dot_general(turned, keys, contract_last, preferred_element_type=f32)

        old = jnp.where(first, scores(k_old[0, :, lanes]), scores(k_old[1, :, lanes]))
        old = jnp.where(valid, old * score_scale, -1e30)
        fresh = scores(k_new[:, lanes]) * score_scale
        other = lax.broadcasted_iota(jnp.int32, fresh.shape, 1)
        keep = (other // 2 == token // 2) & (other <= token)
        fresh = jnp.where(keep, fresh, -1e30)
        highest = jnp.maximum(
            jnp.max(old, axis=1, keepdims=True), jnp.max(fresh, axis=1, keepdims=True)
        )
        old = jnp.exp(old - highest)
        fresh = jnp.exp(fresh - highest)
        denom = jnp.sum(old, axis=1, keepdims=True) + jnp.sum(fresh, axis=1, keepdims=True)
        mixed = (
            dot(jnp.where(first, old, 0.0).astype(bf16), v_old[0, :, lanes])
            + dot(jnp.where(first, 0.0, old).astype(bf16), v_old[1, :, lanes])
            + dot(fresh.astype(bf16), v_new[:, lanes])
        )
        out[mine, :] = (mixed / denom).astype(bf16)


def attend(q, cosine, sine, cache_keys, cache_values, k_new, v_new, lengths):
    step_rows = q.shape[0] // KVH * HEADS_AT_ONCE
    step_cols = HD * HEADS_AT_ONCE
    slots = cache_keys.shape[1]
    fresh_rows = k_new.shape[0]
    return pl.pallas_call(
        attention_kernel,
        out_shape=jax.ShapeDtypeStruct(q.shape, bf16),
        grid_spec=pltpu.PrefetchScalarGridSpec(
            num_scalar_prefetch=1,
            grid=(KVH // HEADS_AT_ONCE,),
            in_specs=[
                pl.BlockSpec((step_rows, HD), lambda g, n: (g, 0)),
                pl.BlockSpec(cosine.shape, lambda g, n: (0, 0)),
                pl.BlockSpec(sine.shape, lambda g, n: (0, 0)),
                pl.BlockSpec((2, slots, step_cols), lambda g, n: (0, 0, g)),
                pl.BlockSpec((2, slots, step_cols), lambda g, n: (0, 0, g)),
                pl.BlockSpec((fresh_rows, step_cols), lambda g, n: (0, g)),
                pl.BlockSpec((fresh_rows, step_cols), lambda g, n: (0, g)),
            ],
            out_specs=pl.BlockSpec((step_rows, HD), lambda g, n: (g, 0)),
        ),
        compiler_params=pltpu.CompilerParams(vmem_limit_bytes=56 * 1024 * 1024),
        cost_estimate=pl.CostEstimate(
            flops=8 * q.shape[0] * slots * HD,
            bytes_accessed=8 * slots * KVH * HD,
            transcendentals=q.shape[0] * slots,
        ),
        name="attention",
    )(lengths, q, cosine, sine, cache_keys, cache_values, k_new, v_new)


LOWER, UPPER = 0, 1
DIRECTIONS = {"z+": ("z", 1), "z-": ("z", -1), "x+": ("x", 1), "x-": ("x", -1), "x2": ("x", 2)}


def tree_rounds():
    a, b = LOWER, UPPER
    return [
        {
            "z+": [(b, 0, 1), (a, 0, 1)],
            "z-": [(b, 0, 7), (a, 0, 7)],
            "x+": [(a, 1, 0), (b, 1, 0)],
            "x-": [(a, 3, 0), (b, 3, 0)],
            "x2": [(a, 2, 0)],
        },
        {
            "z+": [(b, 0, 2), (a, 0, 2), (a, 1, 1), (a, 3, 1), (a, 2, 1)],
            "z-": [(b, 0, 6), (a, 0, 6), (a, 1, 7), (a, 3, 7), (a, 2, 7)],
            "x+": [(b, 1, 1), (b, 1, 7)],
            "x-": [(b, 2, 0), (b, 3, 1), (b, 3, 7)],
        },
        {
            "z+": [(b, 0, 3), (a, 0, 3), (a, 1, 2), (a, 3, 2), (a, 2, 2)],
            "z-": [(b, 0, 5), (a, 0, 5), (a, 1, 6), (a, 3, 6), (a, 2, 6)],
            "x+": [(b, 2, 1), (b, 1, 2), (b, 1, 6)],
            "x-": [(b, 2, 7), (b, 3, 2), (b, 3, 6)],
        },
        {
            "z+": [(a, 0, 4), (a, 1, 3), (a, 3, 3), (a, 2, 3)],
            "z-": [(b, 0, 4), (a, 1, 5), (a, 3, 5), (a, 2, 5)],
            "x+": [(b, 2, 2), (b, 1, 3), (b, 1, 5)],
            "x-": [(b, 2, 6), (b, 3, 3), (b, 3, 5)],
        },
        {
            "z+": [(a, 1, 4), (a, 2, 4)],
            "z-": [(a, 3, 4)],
            "x+": [(b, 2, 3), (b, 1, 4)],
            "x-": [(b, 2, 5), (b, 3, 4)],
            "x2": [(b, 2, 4)],
        },
    ]


def seen_from(item, direction):
    which, dx, dz = item
    axis, sign = DIRECTIONS[direction]
    return (which, (dx - sign) % NX, dz) if axis == "x" else (which, dx, (dz - sign) % NZ)


def gather_rows(piece):
    rows = piece.shape[0] // 2
    messages = [piece]
    places = {(LOWER, 0, 0): (0, 0), (UPPER, 0, 0): (0, rows)}
    for exchange in tree_rounds():
        got = []
        for direction, items in exchange.items():
            held = [places[seen_from(item, direction)] for item in items]
            runs = []
            for message, row in held:
                if runs and runs[-1][0] == message and runs[-1][2] == row:
                    runs[-1][2] += rows
                else:
                    runs.append([message, row, row + rows])
            parts = [messages[m][lo:hi] for m, lo, hi in runs]
            got.append((recv(jnp.concatenate(parts), *DIRECTIONS[direction]), items))
        for message, items in got:
            for k, item in enumerate(items):
                places[item] = (len(messages), k * rows)
            messages.append(message)
    return messages, places


def scatter_rows(terms):
    total = dict(terms)
    for exchange in reversed(tree_rounds()):
        got = []
        for direction, items in exchange.items():
            axis, sign = DIRECTIONS[direction]
            message = jnp.concatenate([total[item] for item in items]).astype(bf16)
            got.append((recv(message, axis, -sign), direction, items))
        arrived = lax.optimization_barrier([message for message, _, _ in got])
        for message, (_, direction, items) in zip(arrived, got):
            rows = message.shape[0] // len(items)
            for k, item in enumerate(items):
                target = seen_from(item, direction)
                total[target] = total[target] + message[k * rows : (k + 1) * rows]
    return total[(LOWER, 0, 0)], total[(UPPER, 0, 0)]


def project(messages, places, w_mine, w_other, w_keyval):
    rows, half = messages[0].shape[0] // 2, messages[0].shape[1]
    block = rows * NZ
    columns = w_mine.shape[1]
    fresh = w_keyval.shape[0] // 2
    part = block + fresh // 2
    count = len(messages)

    def kernel(*refs):
        sources, (mine, other, keyval, out, held) = refs[:count], refs[count:]
        for dx in range(NX):
            for dz in range(NZ):
                for which in (LOWER, UPPER):
                    message, row = places[(which, dx, dz)]
                    to = dx * block + dz * rows
                    held[to : to + rows, which * half : (which + 1) * half] = sources[message][
                        row : row + rows, :
                    ]

        @pl.loop(0, NX)
        def _(dx):
            features = held[pl.ds(pl.multiple_of(dx * block, block), block), :]
            out[dx, :block, :] = dot(features, mine[...])
            out[dx, part : part + block, :] = dot(features, other[...])
            kv = lax.dot_general(
                keyval[...], features, (((1,), (1,)), ((), ())), preferred_element_type=f32
            )
            for core in range(NC):
                top = core * part + block
                for side in range(2):
                    first = core * fresh + side * fresh // 2
                    out[dx, top : top + fresh // 2, side * block : (side + 1) * block] = kv[
                        first : first + fresh // 2
                    ]

    spec = pl.BlockSpec(memory_space=pltpu.VMEM)
    return pl.pallas_call(
        kernel,
        out_shape=jax.ShapeDtypeStruct((NX, 2 * part, columns), f32),
        in_specs=[spec] * (count + 3),
        out_specs=spec,
        scratch_shapes=[pltpu.VMEM((NX * block, 2 * half), bf16)],
        compiler_params=pltpu.CompilerParams(vmem_limit_bytes=32 * 1024 * 1024),
        cost_estimate=pl.CostEstimate(
            flops=8 * NX * block * half * (columns + fresh),
            bytes_accessed=4 * NX * block * half + 8 * half * columns,
            transcendentals=0,
        ),
        name="project",
    )(*messages, w_mine, w_other, w_keyval)


def on_device(
    hidden, norm_gain, w_query, w_keyval, w_out, cache_keys, cache_values, cache_lengths, positions
):
    x, y, z, c = (lax.axis_index(a) for a in "xyzc")
    rows, steps, width = hidden.shape
    tokens = rows * steps
    half = width // 2
    head_cols = w_query.shape[1]
    keyval_cols = w_keyval.shape[2]

    def in_core_order(own, swapped, axis):
        return jnp.where(
            c == 0, jnp.stack([own, swapped], axis=axis), jnp.stack([swapped, own], axis=axis)
        )

    features = hidden.reshape(tokens, width).astype(f32)
    squares = jnp.sum(features * features, axis=-1)
    square_sums = squares + recv(squares, "y", 1) + recv(squares, "y", 2) + recv(squares, "y", 3)
    inverse = lax.rsqrt(square_sums / (width * NY) + norm_epsilon)
    normed = (features * inverse[:, None] * norm_gain.astype(f32)).astype(bf16)
    messages, item_places = gather_rows(jnp.concatenate([normed[:, :half], normed[:, half:]]))

    w_query, w_keyval, w_out, _ = lax.optimization_barrier(
        (w_query, w_keyval, w_out, messages[1])
    )
    w_query_other = recv(w_query, "c", 1)
    w_keyval = w_keyval.transpose(0, 2, 1).reshape(2 * keyval_cols, width)
    w_keyval = jnp.concatenate([w_keyval, recv(w_keyval, "c", 1)])
    w_out_other = recv(w_out, "c", 1)

    places = positions.astype(f32)[:, None] + jnp.arange(steps, dtype=f32)[None, :]
    angles = places.reshape(-1)[:, None] * rope_rates()
    cosine, sine = jnp.cos(angles), jnp.sin(angles)
    cosine = jnp.concatenate([cosine, cosine], axis=1)
    sine = jnp.concatenate([-sine, sine], axis=1)

    partial = project(messages, item_places, w_query, w_query_other, w_keyval)
    block = NZ * tokens

    def block_for(d):
        return lax.dynamic_index_in_dim(partial, (y + d - x + NX) % NX, 0, keepdims=False)

    summed = block_for(0)
    for d in (1, 2, 3):
        summed = summed + recv(block_for(d), "y", -d)
    summed = summed.astype(bf16)
    part = summed.shape[0] // 2
    own, swapped = summed[:part], recv(summed[part:], "c", 1)

    def queries_of(a):
        return a[:block].reshape(NZ, tokens, head_cols)

    def keyvals_of(a):
        a = jnp.concatenate([a[block:, :block], a[block:, block:]])
        return a.T.reshape(NZ, tokens, 2 * keyval_cols)

    back = (NZ - z) % NZ
    q = roll_to(in_core_order(queries_of(own), queries_of(swapped), 1), back)
    kv = roll_to(in_core_order(keyvals_of(own), keyvals_of(swapped), 1), back)
    places_out = 2 * block // TOKENS
    q = q.reshape(places_out, TOKENS, head_cols // HD, HD).transpose(0, 2, 1, 3)
    q = q.reshape(places_out, -1, HD)
    kv = kv.reshape(places_out, 1, -1)
    arrived = lax.all_to_all(
        jnp.concatenate([q, kv], axis=1), ("x", "z", "c"), split_axis=0, concat_axis=0, tiled=True
    )
    q_rows = q.shape[1]
    queries = arrived[:, :q_rows].reshape(-1, HD)
    keyvals = arrived[:, q_rows].reshape(places_out, TOKENS, 2, keyval_cols)
    keyvals = keyvals.transpose(2, 1, 0, 3).reshape(2, TOKENS, KVH, HD)
    fresh_keys = keyvals[0].astype(f32)
    turned_keys = (
        fresh_keys * cosine[:, None] + jnp.roll(fresh_keys, HALF, axis=-1) * sine[:, None]
    ).astype(bf16)
    new = jnp.stack([turned_keys, keyvals[1]]).reshape(2, TOKENS, KVH * HD)
    padded = jnp.pad(new, ((0, 0), (0, 16 - TOKENS), (0, 0)))
    attended = attend(
        queries,
        jnp.tile(cosine, (2, 1)),
        jnp.tile(sine, (2, 1)),
        cache_keys,
        cache_values,
        padded[0],
        padded[1],
        cache_lengths,
    )
    returned = lax.all_to_all(
        attended.reshape(places_out, -1, HD), ("x", "z", "c"), split_axis=0, concat_axis=0, tiled=True
    )
    returned = returned.reshape(places_out, head_cols // HD, TOKENS, HD).transpose(0, 2, 1, 3)
    returned = roll_to(returned.reshape(NZ, NC, tokens, head_cols), z)
    kept = lax.dynamic_index_in_dim(returned, c, 1, keepdims=False)
    got = recv(lax.dynamic_index_in_dim(returned, 1 - c, 1, keepdims=False), "c", 1)
    returned = jnp.stack([kept, got]).reshape(2, block, head_cols)
    line = jnp.stack([returned] + [recv(returned, "y", d) for d in (1, 2, 3)])
    left = [
        lax.dynamic_index_in_dim(line, (x + i - y + NX) % NX, 0, keepdims=False) for i in range(NX)
    ]
    terms = {}
    for dx in (2, 1, 3, 0):
        product = dot(left[dx][0], w_out) + dot(left[dx][1], w_out_other)
        for dz in range(NZ):
            for which in (LOWER, UPPER):
                terms[(which, dx, dz)] = product[
                    dz * tokens : (dz + 1) * tokens, which * half : (which + 1) * half
                ]
    branch = jnp.concatenate(scatter_rows(terms), axis=1).astype(bf16)
    return (
        branch.reshape(rows, steps, width),
        new.reshape(2, TOKENS // steps, steps, KVH * HD),
    )


def solution(mesh):
    fine = Mesh(mesh.devices.reshape(NY, NX, NZ, NC), ("y", "x", "z", "c"))
    gy = ("x", "z", "c")
    everywhere = ("y", "x", "z", "c")
    return jax.shard_map(
        on_device,
        mesh=fine,
        in_specs=(
            P(gy, None, "y"),
            P("y"),
            P("y", gy),
            P(None, "y", gy),
            P(gy, "y"),
            P(everywhere, None, None),
            P(everywhere, None, None),
            P(everywhere),
            P(everywhere),
        ),
        out_specs=(P(gy, None, "y"), P(None, everywhere, None, None)),
        check_vma=False,
    )
```

```python
import math

import jax
import jax.numpy as jnp
from jax import lax
from jax.experimental import pallas as pl
from jax.experimental.pallas import tpu as pltpu
from jax.sharding import Mesh
from jax.sharding import PartitionSpec as P

HQ = 128
KVH = 8
HD = 128
HALF = HD // 2
TOKENS = 4
NX, NY, NZ, NC = 4, 4, 8, 2
f32 = jnp.float32
bf16 = jnp.bfloat16

norm_epsilon = 1e-05


def rope_rates():
    index = jnp.arange(HD // 2, dtype=jnp.float32)
    rates = 1.0 / jnp.power(500000.0, 2.0 * index / HD)
    wavelength = 2.0 * math.pi / rates
    smooth = (8192.0 / wavelength - 1.0) / 3.0
    blended = (1.0 - smooth) * rates / 8.0 + smooth * rates
    return jnp.where(
        wavelength > 8192.0, rates / 8.0, jnp.where(wavelength < 2048.0, rates, blended)
    )


def recv(block, axis, distance):
    size = lax.axis_size(axis)
    return lax.ppermute(block, axis, [((i + distance) % size, i) for i in range(size)])


def roll_to(blocks, start):
    return lax.dynamic_slice_in_dim(
        jnp.concatenate([blocks, blocks], axis=0), start, blocks.shape[0], 0
    )


def dot(a, b):
    return jnp.dot(a, b, preferred_element_type=f32)


HEADS_AT_ONCE = 2


def attention_kernel(lengths, q, cosine, sine, k_old, v_old, k_new, v_new, out):
    rows = q.shape[0] // HEADS_AT_ONCE
    slots = k_old.shape[1]
    repeats = rows // cosine.shape[0]
    cosines = jnp.concatenate([cosine[...]] * repeats)
    sines = jnp.concatenate([sine[...]] * repeats)
    contract_last = (((1,), (1,)), ((), ()))
    score_scale = HD ** (-0.5)
    token = lax.broadcasted_iota(jnp.int32, (rows, 1), 0) % TOKENS
    first = token < 2
    slot = lax.broadcasted_iota(jnp.int32, (rows, slots), 1)
    valid = slot < jnp.where(first, lengths[0], lengths[1])
    for head in range(HEADS_AT_ONCE):
        mine = slice(head * rows, (head + 1) * rows)
        lanes = slice(head * HD, (head + 1) * HD)
        queries = q[mine, :].astype(f32)
        turned = (queries * cosines + pltpu.roll(queries, HALF, 1) * sines).astype(bf16)

        def scores(keys):
            return lax.dot_general(turned, keys, contract_last, preferred_element_type=f32)

        old = jnp.where(first, scores(k_old[0, :, lanes]), scores(k_old[1, :, lanes]))
        old = jnp.where(valid, old * score_scale, -1e30)
        fresh = scores(k_new[:, lanes]) * score_scale
        other = lax.broadcasted_iota(jnp.int32, fresh.shape, 1)
        keep = (other // 2 == token // 2) & (other <= token)
        fresh = jnp.where(keep, fresh, -1e30)
        highest = jnp.maximum(
            jnp.max(old, axis=1, keepdims=True), jnp.max(fresh, axis=1, keepdims=True)
        )
        old = jnp.exp(old - highest)
        fresh = jnp.exp(fresh - highest)
        denom = jnp.sum(old, axis=1, keepdims=True) + jnp.sum(fresh, axis=1, keepdims=True)
        mixed = (
            dot(jnp.where(first, old, 0.0).astype(bf16), v_old[0, :, lanes])
            + dot(jnp.where(first, 0.0, old).astype(bf16), v_old[1, :, lanes])
            + dot(fresh.astype(bf16), v_new[:, lanes])
        )
        out[mine, :] = (mixed / denom).astype(bf16)


def attend(q, cosine, sine, cache_keys, cache_values, k_new, v_new, lengths):
    step_rows = q.shape[0] // KVH * HEADS_AT_ONCE
    step_cols = HD * HEADS_AT_ONCE
    slots = cache_keys.shape[1]
    fresh_rows = k_new.shape[0]
    return pl.pallas_call(
        attention_kernel,
        out_shape=jax.ShapeDtypeStruct(q.shape, bf16),
        grid_spec=pltpu.PrefetchScalarGridSpec(
            num_scalar_prefetch=1,
            grid=(KVH // HEADS_AT_ONCE,),
            in_specs=[
                pl.BlockSpec((step_rows, HD), lambda g, n: (g, 0)),
                pl.BlockSpec(cosine.shape, lambda g, n: (0, 0)),
                pl.BlockSpec(sine.shape, lambda g, n: (0, 0)),
                pl.BlockSpec((2, slots, step_cols), lambda g, n: (0, 0, g)),
                pl.BlockSpec((2, slots, step_cols), lambda g, n: (0, 0, g)),
                pl.BlockSpec((fresh_rows, step_cols), lambda g, n: (0, g)),
                pl.BlockSpec((fresh_rows, step_cols), lambda g, n: (0, g)),
            ],
            out_specs=pl.BlockSpec((step_rows, HD), lambda g, n: (g, 0)),
        ),
        compiler_params=pltpu.CompilerParams(vmem_limit_bytes=56 * 1024 * 1024),
        cost_estimate=pl.CostEstimate(
            flops=8 * q.shape[0] * slots * HD,
            bytes_accessed=8 * slots * KVH * HD,
            transcendentals=q.shape[0] * slots,
        ),
        name="attention",
    )(lengths, q, cosine, sine, cache_keys, cache_values, k_new, v_new)


LOWER, UPPER = 0, 1
DIRECTIONS = {"z+": ("z", 1), "z-": ("z", -1), "x+": ("x", 1), "x-": ("x", -1), "x2": ("x", 2)}


def tree_rounds():
    a, b = LOWER, UPPER
    return [
        {
            "z+": [(a, 0, 1), (b, 0, 1)],
            "z-": [(b, 0, 7), (a, 0, 7)],
            "x+": [(a, 1, 0), (b, 1, 0)],
            "x-": [(a, 3, 0), (b, 3, 0)],
            "x2": [(a, 2, 0)],
        },
        {
            "z+": [(a, 0, 2), (b, 0, 2), (a, 3, 1), (a, 1, 1), (a, 2, 1)],
            "z-": [(b, 0, 6), (a, 0, 6), (a, 1, 7), (a, 2, 7), (a, 3, 7)],
            "x+": [(b, 1, 1), (b, 1, 7)],
            "x-": [(b, 2, 0), (b, 3, 1), (b, 3, 7)],
        },
        {
            "z+": [(a, 0, 3), (b, 0, 3), (a, 3, 2), (a, 1, 2), (a, 2, 2)],
            "z-": [(b, 0, 5), (a, 0, 5), (a, 1, 6), (a, 2, 6), (a, 3, 6)],
            "x+": [(b, 2, 1), (b, 1, 2), (b, 1, 6)],
            "x-": [(b, 2, 7), (b, 3, 2), (b, 3, 6)],
        },
        {
            "z+": [(b, 0, 4), (a, 3, 3), (a, 1, 3), (a, 2, 3)],
            "z-": [(a, 0, 4), (a, 1, 5), (a, 2, 5), (a, 3, 5)],
            "x+": [(b, 2, 2), (b, 1, 3), (b, 1, 5)],
            "x-": [(b, 2, 6), (b, 3, 3), (b, 3, 5)],
        },
        {
            "z+": [(a, 1, 4), (a, 2, 4)],
            "z-": [(a, 3, 4)],
            "x+": [(b, 2, 3), (b, 1, 4)],
            "x-": [(b, 2, 5), (b, 3, 4)],
            "x2": [(b, 2, 4)],
        },
    ]


def seen_from(item, direction):
    which, dx, dz = item
    axis, sign = DIRECTIONS[direction]
    return (which, (dx - sign) % NX, dz) if axis == "x" else (which, dx, (dz - sign) % NZ)


def gather_rows(piece):
    rows = piece.shape[0] // 2
    messages = [piece]
    places = {(LOWER, 0, 0): (0, 0), (UPPER, 0, 0): (0, rows)}
    for exchange in tree_rounds():
        got = []
        for direction, items in exchange.items():
            held = [places[seen_from(item, direction)] for item in items]
            runs = []
            for message, row in held:
                if runs and runs[-1][0] == message and runs[-1][2] == row:
                    runs[-1][2] += rows
                else:
                    runs.append([message, row, row + rows])
            parts = [messages[m][lo:hi] for m, lo, hi in runs]
            message = jnp.concatenate(parts) if len(parts) > 1 else parts[0]
            got.append((recv(message, *DIRECTIONS[direction]), items))
        for message, items in got:
            for k, item in enumerate(items):
                places[item] = (len(messages), k * rows)
            messages.append(message)
    return messages, places


def sums(product, messages, wanted, rows, half):
    used = sorted({m for items in wanted for _, found in items for m, _ in found})
    count = sum(len(items) for items in wanted)

    def kernel(*refs):
        terms, sources = refs[0], dict(zip(used, refs[1 : 1 + len(used)]))
        outs, held, sems = refs[1 + len(used) : -2], refs[-2], refs[-1]
        copies = []
        for items in wanted:
            for (which, dx, dz), _ in items:
                n = len(copies)
                copies.append(
                    pltpu.make_async_copy(
                        terms.at[pl.ds((dx * NZ + dz) * rows, rows), pl.ds(which * half, half)],
                        held.at[n],
                        sems.at[n],
                    )
                )
                copies[-1].start()
        n = 0
        for out, items in zip(outs, wanted):
            for k, (_, found) in enumerate(items):
                copies[n].wait()
                total = held[n]
                for m, row in found:
                    total = total + sources[m][row : row + rows, :].astype(f32)
                out[k * rows : (k + 1) * rows, :] = total.astype(bf16)
                n += 1

    spec = pl.BlockSpec(memory_space=pltpu.VMEM)
    shapes = [jax.ShapeDtypeStruct((len(items) * rows, half), bf16) for items in wanted]
    return pl.pallas_call(
        kernel,
        out_shape=shapes,
        in_specs=[pl.BlockSpec(memory_space=pl.ANY)] + [spec] * len(used),
        out_specs=[spec] * len(shapes),
        scratch_shapes=[
            pltpu.VMEM((count, rows, half), f32),
            pltpu.SemaphoreType.DMA((count,)),
        ],
        compiler_params=pltpu.CompilerParams(vmem_limit_bytes=16 * 1024 * 1024),
        cost_estimate=pl.CostEstimate(
            flops=2 * count * rows * half, bytes_accessed=10 * count * rows * half, transcendentals=0
        ),
        name="sums",
    )(product, *[messages[m] for m in used])


def scatter_rows(product, rows):
    half = product.shape[1] // 2
    messages, found = [], {}
    for exchange in reversed(tree_rounds()):
        wanted = [[(item, found.get(item, [])) for item in items] for items in exchange.values()]
        sent = sums(product, messages, wanted, rows, half)
        got = [
            recv(message, DIRECTIONS[direction][0], -DIRECTIONS[direction][1])
            for direction, message in zip(exchange, sent)
        ]
        got = lax.optimization_barrier(got)
        for message, (direction, items) in zip(got, exchange.items()):
            for k, item in enumerate(items):
                found.setdefault(seen_from(item, direction), []).append((len(messages), k * rows))
            messages.append(message)
    own = [[(item, found[item])] for item in ((LOWER, 0, 0), (UPPER, 0, 0))]
    return jnp.concatenate(sums(product, messages, own, rows, half), axis=1)


def project(messages, places, w_mine, w_other, w_keyval):
    rows, half = messages[0].shape[0] // 2, messages[0].shape[1]
    block = rows * NZ
    columns = w_mine.shape[1]
    fresh = w_keyval.shape[0] // 2
    part = block + fresh // 2
    count = len(messages)
    together = 2

    def kernel(*refs):
        sources, (mine, other, keyval, out, held, sems) = refs[:count], refs[count:]
        copies = []
        for dx in range(NX):
            for dz in range(NZ):
                for which in (LOWER, UPPER):
                    message, row = places[(which, dx, dz)]
                    copies.append(
                        pltpu.make_async_copy(
                            sources[message].at[pl.ds(row, rows), :],
                            held.at[
                                pl.ds(dx * block + dz * rows, rows), pl.ds(which * half, half)
                            ],
                            sems.at[len(copies)],
                        )
                    )
                    copies[-1].start()
        for copy in copies:
            copy.wait()

        @pl.loop(0, NX // together)
        def _(step):
            size = together * block
            features = held[pl.ds(pl.multiple_of(step * size, size), size), :]
            q_mine = dot(features, mine[...])
            q_other = dot(features, other[...])
            kv = lax.dot_general(
                keyval[...], features, (((1,), (1,)), ((), ())), preferred_element_type=f32
            )
            for k in range(together):
                dx = step * together + k
                out[dx, :block, :] = q_mine[k * block : (k + 1) * block]
                out[dx, part : part + block, :] = q_other[k * block : (k + 1) * block]
                for core in range(NC):
                    top = core * part + block
                    for side in range(2):
                        first = core * fresh + side * fresh // 2
                        out[dx, top : top + fresh // 2, side * block : (side + 1) * block] = kv[
                            first : first + fresh // 2, k * block : (k + 1) * block
                        ]

    spec = pl.BlockSpec(memory_space=pltpu.VMEM)
    return pl.pallas_call(
        kernel,
        out_shape=jax.ShapeDtypeStruct((NX, 2 * part, columns), f32),
        in_specs=[pl.BlockSpec(memory_space=pl.ANY)] * count + [spec] * 3,
        out_specs=spec,
        scratch_shapes=[
            pltpu.VMEM((NX * block, 2 * half), bf16),
            pltpu.SemaphoreType.DMA((2 * NX * NZ,)),
        ],
        compiler_params=pltpu.CompilerParams(vmem_limit_bytes=32 * 1024 * 1024),
        cost_estimate=pl.CostEstimate(
            flops=8 * NX * block * half * (columns + fresh),
            bytes_accessed=4 * NX * block * half + 8 * half * columns,
            transcendentals=0,
        ),
        name="project",
    )(*messages, w_mine, w_other, w_keyval)


def on_device(
    hidden, norm_gain, w_query, w_keyval, w_out, cache_keys, cache_values, cache_lengths, positions
):
    x, y, z, c = (lax.axis_index(a) for a in "xyzc")
    rows, steps, width = hidden.shape
    tokens = rows * steps
    half = width // 2
    head_cols = w_query.shape[1]
    keyval_cols = w_keyval.shape[2]

    def in_core_order(own, swapped, axis):
        return jnp.where(
            c == 0, jnp.stack([own, swapped], axis=axis), jnp.stack([swapped, own], axis=axis)
        )

    features = hidden.reshape(tokens, width).astype(f32)
    squares = jnp.sum(features * features, axis=-1)
    square_sums = squares + recv(squares, "y", 1) + recv(squares, "y", 2) + recv(squares, "y", 3)
    inverse = lax.rsqrt(square_sums / (width * NY) + norm_epsilon)
    normed = (features * inverse[:, None] * norm_gain.astype(f32)).astype(bf16)
    messages, item_places = gather_rows(jnp.concatenate([normed[:, :half], normed[:, half:]]))

    w_query, w_keyval, w_out, _ = lax.optimization_barrier(
        (w_query, w_keyval, w_out, messages[1])
    )
    w_query_other = recv(w_query, "c", 1)
    w_keyval = w_keyval.transpose(0, 2, 1).reshape(2 * keyval_cols, width)
    w_keyval = jnp.concatenate([w_keyval, recv(w_keyval, "c", 1)])
    w_out = jnp.concatenate([w_out, recv(w_out, "c", 1)])

    places = positions.astype(f32)[:, None] + jnp.arange(steps, dtype=f32)[None, :]
    angles = places.reshape(-1)[:, None] * rope_rates()
    cosine, sine = jnp.cos(angles), jnp.sin(angles)
    cosine = jnp.concatenate([cosine, cosine], axis=1)
    sine = jnp.concatenate([-sine, sine], axis=1)

    partial = project(messages, item_places, w_query, w_query_other, w_keyval)
    block = NZ * tokens

    def block_for(d):
        return lax.dynamic_index_in_dim(partial, (y + d - x + NX) % NX, 0, keepdims=False)

    summed = block_for(0)
    for d in (1, 2, 3):
        summed = summed + recv(block_for(d), "y", -d)
    summed = summed.astype(bf16)
    part = summed.shape[0] // 2
    own, swapped = summed[:part], recv(summed[part:], "c", 1)

    def queries_of(a):
        return a[:block].reshape(NZ, tokens, head_cols)

    def keyvals_of(a):
        a = jnp.concatenate([a[block:, :block], a[block:, block:]])
        return a.T.reshape(NZ, tokens, 2 * keyval_cols)

    back = (NZ - z) % NZ
    q = roll_to(in_core_order(queries_of(own), queries_of(swapped), 1), back)
    kv = roll_to(in_core_order(keyvals_of(own), keyvals_of(swapped), 1), back)
    places_out = 2 * block // TOKENS
    q = q.reshape(places_out, TOKENS, head_cols // HD, HD).transpose(0, 2, 1, 3)
    q = q.reshape(places_out, -1, HD)
    kv = kv.reshape(places_out, 1, -1)
    arrived = lax.all_to_all(
        jnp.concatenate([q, kv], axis=1), ("x", "z", "c"), split_axis=0, concat_axis=0, tiled=True
    )
    q_rows = q.shape[1]
    queries = arrived[:, :q_rows].reshape(-1, HD)
    keyvals = arrived[:, q_rows].reshape(places_out, TOKENS, 2, keyval_cols)
    keyvals = keyvals.transpose(2, 1, 0, 3).reshape(2, TOKENS, KVH, HD)
    fresh_keys = keyvals[0].astype(f32)
    turned_keys = (
        fresh_keys * cosine[:, None] + jnp.roll(fresh_keys, HALF, axis=-1) * sine[:, None]
    ).astype(bf16)
    new = jnp.stack([turned_keys, keyvals[1]]).reshape(2, TOKENS, KVH * HD)
    padded = jnp.pad(new, ((0, 0), (0, 16 - TOKENS), (0, 0)))
    attended = attend(
        queries,
        jnp.tile(cosine, (2, 1)),
        jnp.tile(sine, (2, 1)),
        cache_keys,
        cache_values,
        padded[0],
        padded[1],
        cache_lengths,
    )
    returned = lax.all_to_all(
        attended.reshape(places_out, -1, HD), ("x", "z", "c"), split_axis=0, concat_axis=0, tiled=True
    )
    returned = returned.reshape(places_out, head_cols // HD, TOKENS, HD).transpose(0, 2, 1, 3)
    returned = roll_to(returned.reshape(NZ, NC, tokens, head_cols), z)
    kept = lax.dynamic_index_in_dim(returned, c, 1, keepdims=False)
    got = recv(lax.dynamic_index_in_dim(returned, 1 - c, 1, keepdims=False), "c", 1)
    returned = jnp.concatenate([kept, got], axis=2).reshape(block, 2 * head_cols)
    line = jnp.stack([returned] + [recv(returned, "y", d) for d in (1, 2, 3)])
    left = jnp.concatenate(
        [
            lax.dynamic_index_in_dim(line, (x + i - y + NX) % NX, 0, keepdims=False)
            for i in range(NX)
        ]
    )
    branch = scatter_rows(dot(left, w_out), tokens)
    return (
        branch.reshape(rows, steps, width),
        new.reshape(2, TOKENS // steps, steps, KVH * HD),
    )


def solution(mesh):
    fine = Mesh(mesh.devices.reshape(NY, NX, NZ, NC), ("y", "x", "z", "c"))
    gy = ("x", "z", "c")
    everywhere = ("y", "x", "z", "c")
    return jax.shard_map(
        on_device,
        mesh=fine,
        in_specs=(
            P(gy, None, "y"),
            P("y"),
            P("y", gy),
            P(None, "y", gy),
            P(gy, "y"),
            P(everywhere, None, None),
            P(everywhere, None, None),
            P(everywhere),
            P(everywhere),
        ),
        out_specs=(P(gy, None, "y"), P(None, everywhere, None, None)),
        check_vma=False,
    )
```

```python
import math

import jax
import jax.numpy as jnp
from jax import lax
from jax.experimental import pallas as pl
from jax.experimental.pallas import tpu as pltpu
from jax.sharding import Mesh
from jax.sharding import PartitionSpec as P

HQ = 128
KVH = 8
HD = 128
HALF = HD // 2
TOKENS = 4
NX, NY, NZ, NC = 4, 4, 8, 2
f32 = jnp.float32
bf16 = jnp.bfloat16

norm_epsilon = 1e-05


def rope_rates():
    index = jnp.arange(HD // 2, dtype=jnp.float32)
    rates = 1.0 / jnp.power(500000.0, 2.0 * index / HD)
    wavelength = 2.0 * math.pi / rates
    smooth = (8192.0 / wavelength - 1.0) / 3.0
    blended = (1.0 - smooth) * rates / 8.0 + smooth * rates
    return jnp.where(
        wavelength > 8192.0, rates / 8.0, jnp.where(wavelength < 2048.0, rates, blended)
    )


def recv(block, axis, distance):
    size = lax.axis_size(axis)
    return lax.ppermute(block, axis, [((i + distance) % size, i) for i in range(size)])


def roll_to(blocks, start):
    return lax.dynamic_slice_in_dim(
        jnp.concatenate([blocks, blocks], axis=0), start, blocks.shape[0], 0
    )


def dot(a, b):
    return jnp.dot(a, b, preferred_element_type=f32)


HEADS_AT_ONCE = 2


def attention_kernel(lengths, q, cosine, sine, k_old, v_old, k_new, v_new, out):
    rows = q.shape[0] // HEADS_AT_ONCE
    slots = k_old.shape[1]
    repeats = rows // cosine.shape[0]
    cosines = jnp.concatenate([cosine[...]] * repeats)
    sines = jnp.concatenate([sine[...]] * repeats)
    contract_last = (((1,), (1,)), ((), ()))
    score_scale = HD ** (-0.5)
    token = lax.broadcasted_iota(jnp.int32, (rows, 1), 0) % TOKENS
    first = token < 2
    slot = lax.broadcasted_iota(jnp.int32, (rows, slots), 1)
    valid = slot < jnp.where(first, lengths[0], lengths[1])
    for head in range(HEADS_AT_ONCE):
        mine = slice(head * rows, (head + 1) * rows)
        lanes = slice(head * HD, (head + 1) * HD)
        queries = q[mine, :].astype(f32)
        turned = (queries * cosines + pltpu.roll(queries, HALF, 1) * sines).astype(bf16)

        def scores(keys):
            return lax.dot_general(turned, keys, contract_last, preferred_element_type=f32)

        old = jnp.where(first, scores(k_old[0, :, lanes]), scores(k_old[1, :, lanes]))
        old = jnp.where(valid, old * score_scale, -1e30)
        fresh = scores(k_new[:, lanes]) * score_scale
        other = lax.broadcasted_iota(jnp.int32, fresh.shape, 1)
        keep = (other // 2 == token // 2) & (other <= token)
        fresh = jnp.where(keep, fresh, -1e30)
        highest = jnp.maximum(
            jnp.max(old, axis=1, keepdims=True), jnp.max(fresh, axis=1, keepdims=True)
        )
        old = jnp.exp(old - highest)
        fresh = jnp.exp(fresh - highest)
        denom = jnp.sum(old, axis=1, keepdims=True) + jnp.sum(fresh, axis=1, keepdims=True)
        mixed = (
            dot(jnp.where(first, old, 0.0).astype(bf16), v_old[0, :, lanes])
            + dot(jnp.where(first, 0.0, old).astype(bf16), v_old[1, :, lanes])
            + dot(fresh.astype(bf16), v_new[:, lanes])
        )
        out[mine, :] = (mixed / denom).astype(bf16)


def attend(q, cosine, sine, cache_keys, cache_values, new, lengths):
    step_rows = q.shape[0] // KVH * HEADS_AT_ONCE
    step_cols = HD * HEADS_AT_ONCE
    slots = cache_keys.shape[1]
    fresh_rows = new.shape[1]
    return pl.pallas_call(
        attention_kernel,
        out_shape=jax.ShapeDtypeStruct(q.shape, bf16),
        grid_spec=pltpu.PrefetchScalarGridSpec(
            num_scalar_prefetch=1,
            grid=(KVH // HEADS_AT_ONCE,),
            in_specs=[
                pl.BlockSpec((step_rows, HD), lambda g, n: (g, 0)),
                pl.BlockSpec(cosine.shape, lambda g, n: (0, 0)),
                pl.BlockSpec(sine.shape, lambda g, n: (0, 0)),
                pl.BlockSpec((2, slots, step_cols), lambda g, n: (0, 0, g)),
                pl.BlockSpec((2, slots, step_cols), lambda g, n: (0, 0, g)),
                pl.BlockSpec((None, fresh_rows, step_cols), lambda g, n: (0, 0, g)),
                pl.BlockSpec((None, fresh_rows, step_cols), lambda g, n: (1, 0, g)),
            ],
            out_specs=pl.BlockSpec((step_rows, HD), lambda g, n: (g, 0)),
        ),
        compiler_params=pltpu.CompilerParams(vmem_limit_bytes=56 * 1024 * 1024),
        cost_estimate=pl.CostEstimate(
            flops=8 * q.shape[0] * slots * HD,
            bytes_accessed=8 * slots * KVH * HD,
            transcendentals=q.shape[0] * slots,
        ),
        name="attention",
    )(lengths, q, cosine, sine, cache_keys, cache_values, new, new)


LOWER, UPPER = 0, 1
DIRECTIONS = {"z+": ("z", 1), "z-": ("z", -1), "x+": ("x", 1), "x-": ("x", -1), "x2": ("x", 2)}


def tree_rounds():
    a, b = LOWER, UPPER
    return [
        {
            "z+": [(a, 0, 1), (b, 0, 1)],
            "z-": [(b, 0, 7), (a, 0, 7)],
            "x+": [(a, 1, 0), (b, 1, 0)],
            "x-": [(a, 3, 0), (b, 3, 0)],
            "x2": [(a, 2, 0)],
        },
        {
            "z+": [(a, 0, 2), (b, 0, 2), (a, 3, 1), (a, 1, 1), (a, 2, 1)],
            "z-": [(b, 0, 6), (a, 0, 6), (a, 1, 7), (a, 2, 7), (a, 3, 7)],
            "x+": [(b, 1, 1), (b, 1, 7)],
            "x-": [(b, 2, 0), (b, 3, 1), (b, 3, 7)],
        },
        {
            "z+": [(a, 0, 3), (b, 0, 3), (a, 3, 2), (a, 1, 2), (a, 2, 2)],
            "z-": [(b, 0, 5), (a, 0, 5), (a, 1, 6), (a, 2, 6), (a, 3, 6)],
            "x+": [(b, 2, 1), (b, 1, 2), (b, 1, 6)],
            "x-": [(b, 2, 7), (b, 3, 2), (b, 3, 6)],
        },
        {
            "z+": [(b, 0, 4), (a, 3, 3), (a, 1, 3), (a, 2, 3)],
            "z-": [(a, 0, 4), (a, 1, 5), (a, 2, 5), (a, 3, 5)],
            "x+": [(b, 2, 2), (b, 1, 3), (b, 1, 5)],
            "x-": [(b, 2, 6), (b, 3, 3), (b, 3, 5)],
        },
        {
            "z+": [(a, 1, 4), (a, 2, 4)],
            "z-": [(a, 3, 4)],
            "x+": [(b, 2, 3), (b, 1, 4)],
            "x-": [(b, 2, 5), (b, 3, 4)],
            "x2": [(b, 2, 4)],
        },
    ]


def seen_from(item, direction):
    which, dx, dz = item
    axis, sign = DIRECTIONS[direction]
    return (which, (dx - sign) % NX, dz) if axis == "x" else (which, dx, (dz - sign) % NZ)


def gather_rows(piece, aside):
    rows = piece.shape[0] // 2
    messages = [piece]
    places = {(LOWER, 0, 0): (0, 0), (UPPER, 0, 0): (0, rows)}
    for number, exchange in enumerate(tree_rounds()):
        if number == 2:
            messages[-1], aside = lax.optimization_barrier((messages[-1], aside))
        got = []
        for direction, items in exchange.items():
            held = [places[seen_from(item, direction)] for item in items]
            runs = []
            for message, row in held:
                if runs and runs[-1][0] == message and runs[-1][2] == row:
                    runs[-1][2] += rows
                else:
                    runs.append([message, row, row + rows])
            parts = [messages[m][lo:hi] for m, lo, hi in runs]
            message = jnp.concatenate(parts) if len(parts) > 1 else parts[0]
            got.append((recv(message, *DIRECTIONS[direction]), items))
        for message, items in got:
            for k, item in enumerate(items):
                places[item] = (len(messages), k * rows)
            messages.append(message)
    return messages, places, aside


def sums(product, messages, wanted, rows, half):
    used = sorted({m for items in wanted for _, found in items for m, _ in found})
    count = sum(len(items) for items in wanted)

    def kernel(*refs):
        terms, sources = refs[0], dict(zip(used, refs[1 : 1 + len(used)]))
        outs, held, sems = refs[1 + len(used) : -2], refs[-2], refs[-1]
        copies = []
        for items in wanted:
            for (which, dx, dz), _ in items:
                n = len(copies)
                copies.append(
                    pltpu.make_async_copy(
                        terms.at[pl.ds((dx * NZ + dz) * rows, rows), pl.ds(which * half, half)],
                        held.at[n],
                        sems.at[n],
                    )
                )
                copies[-1].start()
        n = 0
        for out, items in zip(outs, wanted):
            for k, (_, found) in enumerate(items):
                copies[n].wait()
                total = held[n]
                for m, row in found:
                    total = total + sources[m][row : row + rows, :].astype(f32)
                out[k * rows : (k + 1) * rows, :] = total.astype(bf16)
                n += 1

    spec = pl.BlockSpec(memory_space=pltpu.VMEM)
    shapes = [jax.ShapeDtypeStruct((len(items) * rows, half), bf16) for items in wanted]
    return pl.pallas_call(
        kernel,
        out_shape=shapes,
        in_specs=[pl.BlockSpec(memory_space=pltpu.HBM)] + [spec] * len(used),
        out_specs=[spec] * len(shapes),
        scratch_shapes=[
            pltpu.VMEM((count, rows, half), f32),
            pltpu.SemaphoreType.DMA((count,)),
        ],
        compiler_params=pltpu.CompilerParams(vmem_limit_bytes=16 * 1024 * 1024),
        cost_estimate=pl.CostEstimate(
            flops=2 * count * rows * half, bytes_accessed=10 * count * rows * half, transcendentals=0
        ),
        name="sums",
    )(product, *[messages[m] for m in used])


def scatter_rows(product, rows):
    half = product.shape[1] // 2
    messages, found = [], {}
    for exchange in reversed(tree_rounds()):
        wanted = [[(item, found.get(item, [])) for item in items] for items in exchange.values()]
        sent = sums(product, messages, wanted, rows, half)
        got = [
            recv(message, DIRECTIONS[direction][0], -DIRECTIONS[direction][1])
            for direction, message in zip(exchange, sent)
        ]
        got = lax.optimization_barrier(got)
        for message, (direction, items) in zip(got, exchange.items()):
            for k, item in enumerate(items):
                found.setdefault(seen_from(item, direction), []).append((len(messages), k * rows))
            messages.append(message)
    own = [[(item, found[item])] for item in ((LOWER, 0, 0), (UPPER, 0, 0))]
    return jnp.concatenate(sums(product, messages, own, rows, half), axis=1)


def project(messages, places, w_mine, w_other, w_keyval):
    rows, half = messages[0].shape[0] // 2, messages[0].shape[1]
    block = rows * NZ
    columns = w_mine.shape[1]
    fresh = w_keyval.shape[0] // 2
    part = block + fresh // 2
    count = len(messages)
    together = 2

    def kernel(*refs):
        sources, (mine, other, keyval, out, held) = refs[:count], refs[count:]
        for dx in range(NX):
            for dz in range(NZ):
                for which in (LOWER, UPPER):
                    message, row = places[(which, dx, dz)]
                    to = dx * block + dz * rows
                    held[to : to + rows, which * half : (which + 1) * half] = sources[message][
                        row : row + rows, :
                    ]

        @pl.loop(0, NX // together)
        def _(step):
            size = together * block
            features = held[pl.ds(pl.multiple_of(step * size, size), size), :]
            q_mine = dot(features, mine[...])
            q_other = dot(features, other[...])
            kv = lax.dot_general(
                keyval[...], features, (((1,), (1,)), ((), ())), preferred_element_type=f32
            )
            for k in range(together):
                dx = step * together + k
                out[dx, :block, :] = q_mine[k * block : (k + 1) * block]
                out[dx, part : part + block, :] = q_other[k * block : (k + 1) * block]
                for core in range(NC):
                    top = core * part + block
                    for side in range(2):
                        first = core * fresh + side * fresh // 2
                        out[dx, top : top + fresh // 2, side * block : (side + 1) * block] = kv[
                            first : first + fresh // 2, k * block : (k + 1) * block
                        ]

    spec = pl.BlockSpec(memory_space=pltpu.VMEM)
    return pl.pallas_call(
        kernel,
        out_shape=jax.ShapeDtypeStruct((NX, 2 * part, columns), f32),
        in_specs=[spec] * (count + 3),
        out_specs=spec,
        scratch_shapes=[pltpu.VMEM((NX * block, 2 * half), bf16)],
        compiler_params=pltpu.CompilerParams(vmem_limit_bytes=16 * 1024 * 1024),
        cost_estimate=pl.CostEstimate(
            flops=8 * NX * block * half * (columns + fresh),
            bytes_accessed=4 * NX * block * half + 8 * half * columns,
            transcendentals=0,
        ),
        name="project",
    )(*messages, w_mine, w_other, w_keyval)


def on_device(
    hidden, norm_gain, w_query, w_keyval, w_out, cache_keys, cache_values, cache_lengths, positions
):
    x, y, z, c = (lax.axis_index(a) for a in "xyzc")
    rows, steps, width = hidden.shape
    tokens = rows * steps
    half = width // 2
    head_cols = w_query.shape[1]
    keyval_cols = w_keyval.shape[2]

    def in_core_order(own, swapped, axis):
        return jnp.where(
            c == 0, jnp.stack([own, swapped], axis=axis), jnp.stack([swapped, own], axis=axis)
        )

    features = hidden.reshape(tokens, width).astype(f32)
    squares = jnp.sum(features * features, axis=-1)
    square_sums = squares + recv(squares, "y", 1) + recv(squares, "y", 2) + recv(squares, "y", 3)
    inverse = lax.rsqrt(square_sums / (width * NY) + norm_epsilon)
    normed = (features * inverse[:, None] * norm_gain.astype(f32)).astype(bf16)
    places = positions.astype(f32)[:, None] + jnp.arange(steps, dtype=f32)[None, :]
    angles = places.reshape(-1)[:, None] * rope_rates()
    cosine, sine = jnp.cos(angles), jnp.sin(angles)
    cosine = jnp.concatenate([cosine, cosine], axis=1)
    sine = jnp.concatenate([-sine, sine], axis=1)
    tables = (jnp.tile(cosine, (2, 1)), jnp.tile(sine, (2, 1)))
    messages, item_places, tables = gather_rows(
        jnp.concatenate([normed[:, :half], normed[:, half:]]), tables
    )
    cosine, sine = tables[0][:TOKENS], tables[1][:TOKENS]

    w_query, w_keyval, w_out, _ = lax.optimization_barrier(
        (w_query, w_keyval, w_out, messages[1])
    )
    w_query_other = recv(w_query, "c", 1)
    w_keyval = w_keyval.transpose(0, 2, 1).reshape(2 * keyval_cols, width)
    w_keyval = jnp.concatenate([w_keyval, recv(w_keyval, "c", 1)])
    w_out = jnp.concatenate([w_out, recv(w_out, "c", 1)])

    partial = project(messages, item_places, w_query, w_query_other, w_keyval)
    block = NZ * tokens

    def block_for(d):
        return lax.dynamic_index_in_dim(partial, (y + d - x + NX) % NX, 0, keepdims=False)

    summed = block_for(0)
    for d in (1, 2, 3):
        summed = summed + recv(block_for(d), "y", -d)
    summed = summed.astype(bf16)
    part = summed.shape[0] // 2
    own, swapped = summed[:part], recv(summed[part:], "c", 1)

    def queries_of(a):
        return a[:block].reshape(NZ, tokens, head_cols)

    def keyvals_of(a):
        a = jnp.concatenate([a[block:, :block], a[block:, block:]])
        return a.T.reshape(NZ, tokens, 2 * keyval_cols)

    back = (NZ - z) % NZ
    q = roll_to(in_core_order(queries_of(own), queries_of(swapped), 1), back)
    kv = roll_to(in_core_order(keyvals_of(own), keyvals_of(swapped), 1), back)
    places_out = 2 * block // TOKENS
    q = q.reshape(places_out, TOKENS, head_cols // HD, HD).transpose(0, 2, 1, 3)
    q = q.reshape(places_out, -1, HD)
    kv = kv.reshape(places_out, 1, -1)
    arrived = lax.all_to_all(
        jnp.concatenate([q, kv], axis=1), ("x", "z", "c"), split_axis=0, concat_axis=0, tiled=True
    )
    q_rows = q.shape[1]
    queries = arrived[:, :q_rows].reshape(-1, HD)
    keyvals = arrived[:, q_rows].reshape(places_out, TOKENS, 2, keyval_cols)
    keyvals = keyvals.transpose(2, 1, 0, 3).reshape(2, TOKENS, KVH, HD)
    fresh_keys = keyvals[0].astype(f32)
    turned_keys = (
        fresh_keys * cosine[:, None] + jnp.roll(fresh_keys, HALF, axis=-1) * sine[:, None]
    ).astype(bf16)
    new = jnp.stack([turned_keys, keyvals[1]]).reshape(2, TOKENS, KVH * HD)
    padded = jnp.pad(new, ((0, 0), (0, 16 - TOKENS), (0, 0)))
    attended = attend(
        queries,
        *tables,
        cache_keys,
        cache_values,
        padded,
        cache_lengths,
    )
    returned = lax.all_to_all(
        attended.reshape(places_out, -1, HD), ("x", "z", "c"), split_axis=0, concat_axis=0, tiled=True
    )
    returned = returned.reshape(places_out, head_cols // HD, TOKENS, HD).transpose(0, 2, 1, 3)
    returned = roll_to(returned.reshape(NZ, NC, tokens, head_cols), z)
    kept = lax.dynamic_index_in_dim(returned, c, 1, keepdims=False)
    got = recv(lax.dynamic_index_in_dim(returned, 1 - c, 1, keepdims=False), "c", 1)
    returned = jnp.concatenate([kept, got], axis=2).reshape(block, 2 * head_cols)
    line = jnp.stack([returned] + [recv(returned, "y", d) for d in (1, 2, 3)])
    left = jnp.concatenate(
        [
            lax.dynamic_index_in_dim(line, (x + i - y + NX) % NX, 0, keepdims=False)
            for i in range(NX)
        ]
    )
    branch = scatter_rows(dot(left, w_out), tokens)
    return (
        branch.reshape(rows, steps, width),
        new.reshape(2, TOKENS // steps, steps, KVH * HD),
    )


def solution(mesh):
    fine = Mesh(mesh.devices.reshape(NY, NX, NZ, NC), ("y", "x", "z", "c"))
    gy = ("x", "z", "c")
    everywhere = ("y", "x", "z", "c")
    return jax.shard_map(
        on_device,
        mesh=fine,
        in_specs=(
            P(gy, None, "y"),
            P("y"),
            P("y", gy),
            P(None, "y", gy),
            P(gy, "y"),
            P(everywhere, None, None),
            P(everywhere, None, None),
            P(everywhere),
            P(everywhere),
        ),
        out_specs=(P(gy, None, "y"), P(None, everywhere, None, None)),
        check_vma=False,
    )
```

```python
import math

import jax
import jax.numpy as jnp
from jax import lax
from jax.experimental import pallas as pl
from jax.experimental.pallas import tpu as pltpu
from jax.sharding import Mesh
from jax.sharding import PartitionSpec as P

HQ = 128
KVH = 8
HD = 128
HALF = HD // 2
TOKENS = 4
NX, NY, NZ, NC = 4, 4, 8, 2
f32 = jnp.float32
bf16 = jnp.bfloat16

norm_epsilon = 1e-05


def rope_rates():
    index = jnp.arange(HD // 2, dtype=jnp.float32)
    rates = 1.0 / jnp.power(500000.0, 2.0 * index / HD)
    wavelength = 2.0 * math.pi / rates
    smooth = (8192.0 / wavelength - 1.0) / 3.0
    blended = (1.0 - smooth) * rates / 8.0 + smooth * rates
    return jnp.where(
        wavelength > 8192.0, rates / 8.0, jnp.where(wavelength < 2048.0, rates, blended)
    )


def recv(block, axis, distance):
    size = lax.axis_size(axis)
    return lax.ppermute(block, axis, [((i + distance) % size, i) for i in range(size)])


def roll_to(blocks, start):
    return lax.dynamic_slice_in_dim(
        jnp.concatenate([blocks, blocks], axis=0), start, blocks.shape[0], 0
    )


def dot(a, b):
    return jnp.dot(a, b, preferred_element_type=f32)


HEADS_AT_ONCE = 2


def attention_kernel(lengths, q, cosine, sine, k_old, v_old, k_new, v_new, out):
    rows = q.shape[0] // HEADS_AT_ONCE
    slots = k_old.shape[1]
    repeats = rows // cosine.shape[0]
    cosines = jnp.concatenate([cosine[...]] * repeats)
    sines = jnp.concatenate([sine[...]] * repeats)
    contract_last = (((1,), (1,)), ((), ()))
    score_scale = HD ** (-0.5)
    token = lax.broadcasted_iota(jnp.int32, (rows, 1), 0) % TOKENS
    first = token < 2
    slot = lax.broadcasted_iota(jnp.int32, (rows, slots), 1)
    valid = slot < jnp.where(first, lengths[0], lengths[1])
    for head in range(HEADS_AT_ONCE):
        mine = slice(head * rows, (head + 1) * rows)
        lanes = slice(head * HD, (head + 1) * HD)
        queries = q[mine, :].astype(f32)
        turned = (queries * cosines + pltpu.roll(queries, HALF, 1) * sines).astype(bf16)

        def scores(keys):
            return lax.dot_general(turned, keys, contract_last, preferred_element_type=f32)

        old = jnp.where(first, scores(k_old[0, :, lanes]), scores(k_old[1, :, lanes]))
        old = jnp.where(valid, old * score_scale, -1e30)
        fresh = scores(k_new[:, lanes]) * score_scale
        other = lax.broadcasted_iota(jnp.int32, fresh.shape, 1)
        keep = (other // 2 == token // 2) & (other <= token)
        fresh = jnp.where(keep, fresh, -1e30)
        highest = jnp.maximum(
            jnp.max(old, axis=1, keepdims=True), jnp.max(fresh, axis=1, keepdims=True)
        )
        old = jnp.exp(old - highest)
        fresh = jnp.exp(fresh - highest)
        denom = jnp.sum(old, axis=1, keepdims=True) + jnp.sum(fresh, axis=1, keepdims=True)
        mixed = (
            dot(jnp.where(first, old, 0.0).astype(bf16), v_old[0, :, lanes])
            + dot(jnp.where(first, 0.0, old).astype(bf16), v_old[1, :, lanes])
            + dot(fresh.astype(bf16), v_new[:, lanes])
        )
        out[mine, :] = (mixed / denom).astype(bf16)


def attend(q, cosine, sine, cache_keys, cache_values, new, lengths):
    step_rows = q.shape[0] // KVH * HEADS_AT_ONCE
    step_cols = HD * HEADS_AT_ONCE
    slots = cache_keys.shape[1]
    fresh_rows = new.shape[1]
    return pl.pallas_call(
        attention_kernel,
        out_shape=jax.ShapeDtypeStruct(q.shape, bf16),
        grid_spec=pltpu.PrefetchScalarGridSpec(
            num_scalar_prefetch=1,
            grid=(KVH // HEADS_AT_ONCE,),
            in_specs=[
                pl.BlockSpec((step_rows, HD), lambda g, n: (g, 0)),
                pl.BlockSpec(cosine.shape, lambda g, n: (0, 0)),
                pl.BlockSpec(sine.shape, lambda g, n: (0, 0)),
                pl.BlockSpec((2, slots, step_cols), lambda g, n: (0, 0, g)),
                pl.BlockSpec((2, slots, step_cols), lambda g, n: (0, 0, g)),
                pl.BlockSpec((None, fresh_rows, step_cols), lambda g, n: (0, 0, g)),
                pl.BlockSpec((None, fresh_rows, step_cols), lambda g, n: (1, 0, g)),
            ],
            out_specs=pl.BlockSpec((step_rows, HD), lambda g, n: (g, 0)),
        ),
        compiler_params=pltpu.CompilerParams(vmem_limit_bytes=56 * 1024 * 1024),
        cost_estimate=pl.CostEstimate(
            flops=8 * q.shape[0] * slots * HD,
            bytes_accessed=8 * slots * KVH * HD,
            transcendentals=q.shape[0] * slots,
        ),
        name="attention",
    )(lengths, q, cosine, sine, cache_keys, cache_values, new, new)


LOWER, UPPER = 0, 1
DIRECTIONS = {"z+": ("z", 1), "z-": ("z", -1), "x+": ("x", 1), "x-": ("x", -1), "x2": ("x", 2)}


def tree_rounds():
    a, b = LOWER, UPPER
    return [
        {
            "z+": [(a, 0, 1), (b, 0, 1)],
            "z-": [(b, 0, 7), (a, 0, 7)],
            "x+": [(a, 1, 0), (b, 1, 0)],
            "x-": [(a, 3, 0), (b, 3, 0)],
            "x2": [(a, 2, 0)],
        },
        {
            "z+": [(a, 0, 2), (b, 0, 2), (a, 3, 1), (a, 1, 1), (a, 2, 1)],
            "z-": [(b, 0, 6), (a, 0, 6), (a, 1, 7), (a, 2, 7), (a, 3, 7)],
            "x+": [(b, 1, 1), (b, 1, 7)],
            "x-": [(b, 2, 0), (b, 3, 1), (b, 3, 7)],
        },
        {
            "z+": [(a, 0, 3), (b, 0, 3), (a, 3, 2), (a, 1, 2), (a, 2, 2)],
            "z-": [(b, 0, 5), (a, 0, 5), (a, 1, 6), (a, 2, 6), (a, 3, 6)],
            "x+": [(b, 2, 1), (b, 1, 2), (b, 1, 6)],
            "x-": [(b, 2, 7), (b, 3, 2), (b, 3, 6)],
        },
        {
            "z+": [(b, 0, 4), (a, 3, 3), (a, 1, 3), (a, 2, 3)],
            "z-": [(a, 0, 4), (a, 1, 5), (a, 2, 5), (a, 3, 5)],
            "x+": [(b, 2, 2), (b, 1, 3), (b, 1, 5)],
            "x-": [(b, 2, 6), (b, 3, 3), (b, 3, 5)],
        },
        {
            "z+": [(a, 1, 4), (a, 2, 4)],
            "z-": [(a, 3, 4)],
            "x+": [(b, 2, 3), (b, 1, 4)],
            "x-": [(b, 2, 5), (b, 3, 4)],
            "x2": [(b, 2, 4)],
        },
    ]


def seen_from(item, direction):
    which, dx, dz = item
    axis, sign = DIRECTIONS[direction]
    return (which, (dx - sign) % NX, dz) if axis == "x" else (which, dx, (dz - sign) % NZ)


def gather_rows(piece, aside):
    rows = piece.shape[0] // 2
    messages = [piece]
    places = {(LOWER, 0, 0): (0, 0), (UPPER, 0, 0): (0, rows)}
    for number, exchange in enumerate(tree_rounds()):
        if number == 2:
            messages[-1], aside = lax.optimization_barrier((messages[-1], aside))
        got = []
        for direction, items in exchange.items():
            held = [places[seen_from(item, direction)] for item in items]
            runs = []
            for message, row in held:
                if runs and runs[-1][0] == message and runs[-1][2] == row:
                    runs[-1][2] += rows
                else:
                    runs.append([message, row, row + rows])
            parts = [messages[m][lo:hi] for m, lo, hi in runs]
            message = jnp.concatenate(parts) if len(parts) > 1 else parts[0]
            got.append((recv(message, *DIRECTIONS[direction]), items))
        for message, items in got:
            for k, item in enumerate(items):
                places[item] = (len(messages), k * rows)
            messages.append(message)
    return messages, places, aside


def sums(product, messages, wanted, rows, half):
    used = sorted({m for items in wanted for _, found in items for m, _ in found})
    count = sum(len(items) for items in wanted)

    def kernel(*refs):
        terms, sources = refs[0], dict(zip(used, refs[1 : 1 + len(used)]))
        outs, held, sems = refs[1 + len(used) : -2], refs[-2], refs[-1]
        copies = []
        for items in wanted:
            for (which, dx, dz), _ in items:
                n = len(copies)
                copies.append(
                    pltpu.make_async_copy(
                        terms.at[pl.ds((dx * NZ + dz) * rows, rows), pl.ds(which * half, half)],
                        held.at[n],
                        sems.at[n],
                    )
                )
                copies[-1].start()
        n = 0
        for out, items in zip(outs, wanted):
            for k, (_, found) in enumerate(items):
                copies[n].wait()
                total = held[n]
                for m, row in found:
                    total = total + sources[m][row : row + rows, :].astype(f32)
                out[k * rows : (k + 1) * rows, :] = total.astype(bf16)
                n += 1

    spec = pl.BlockSpec(memory_space=pltpu.VMEM)
    shapes = [jax.ShapeDtypeStruct((len(items) * rows, half), bf16) for items in wanted]
    return pl.pallas_call(
        kernel,
        out_shape=shapes,
        in_specs=[pl.BlockSpec(memory_space=pl.ANY)] + [spec] * len(used),
        out_specs=[spec] * len(shapes),
        scratch_shapes=[
            pltpu.VMEM((count, rows, half), f32),
            pltpu.SemaphoreType.DMA((count,)),
        ],
        compiler_params=pltpu.CompilerParams(vmem_limit_bytes=16 * 1024 * 1024),
        cost_estimate=pl.CostEstimate(
            flops=2 * count * rows * half, bytes_accessed=10 * count * rows * half, transcendentals=0
        ),
        name="sums",
    )(product, *[messages[m] for m in used])


def scatter_rows(product, rows):
    half = product.shape[1] // 2
    messages, found = [], {}
    for exchange in reversed(tree_rounds()):
        wanted = [[(item, found.get(item, [])) for item in items] for items in exchange.values()]
        sent = sums(product, messages, wanted, rows, half)
        got = [
            recv(message, DIRECTIONS[direction][0], -DIRECTIONS[direction][1])
            for direction, message in zip(exchange, sent)
        ]
        got = lax.optimization_barrier(got)
        for message, (direction, items) in zip(got, exchange.items()):
            for k, item in enumerate(items):
                found.setdefault(seen_from(item, direction), []).append((len(messages), k * rows))
            messages.append(message)
    own = [[(item, found[item])] for item in ((LOWER, 0, 0), (UPPER, 0, 0))]
    return jnp.concatenate(sums(product, messages, own, rows, half), axis=1)


def project(messages, places, w_mine, w_other, w_keyval):
    rows, half = messages[0].shape[0] // 2, messages[0].shape[1]
    block = rows * NZ
    columns = w_mine.shape[1]
    fresh = w_keyval.shape[0] // 2
    part = block + fresh // 2
    count = len(messages)
    together = 2

    def kernel(*refs):
        sources, weights = refs[:count], refs[count : count + 3]
        out, held, mine, other, keyval, sems = refs[count + 3 :]
        copies = []

        def fetch(source, target):
            copies.append(pltpu.make_async_copy(source, target, sems.at[len(copies)]))
            copies[-1].start()

        for dx in range(NX):
            for dz in range(NZ):
                for which in (LOWER, UPPER):
                    message, row = places[(which, dx, dz)]
                    fetch(
                        sources[message].at[pl.ds(row, rows), :],
                        held.at[pl.ds(dx * block + dz * rows, rows), pl.ds(which * half, half)],
                    )
        for source, target in zip(weights, (mine, other, keyval)):
            fetch(source, target)
        for copy in copies:
            copy.wait()

        @pl.loop(0, NX // together)
        def _(step):
            size = together * block
            features = held[pl.ds(pl.multiple_of(step * size, size), size), :]
            q_mine = dot(features, mine[...])
            q_other = dot(features, other[...])
            kv = lax.dot_general(
                keyval[...], features, (((1,), (1,)), ((), ())), preferred_element_type=f32
            )
            for k in range(together):
                dx = step * together + k
                out[dx, :block, :] = q_mine[k * block : (k + 1) * block]
                out[dx, part : part + block, :] = q_other[k * block : (k + 1) * block]
                for core in range(NC):
                    top = core * part + block
                    for side in range(2):
                        first = core * fresh + side * fresh // 2
                        out[dx, top : top + fresh // 2, side * block : (side + 1) * block] = kv[
                            first : first + fresh // 2, k * block : (k + 1) * block
                        ]

    spec = pl.BlockSpec(memory_space=pltpu.VMEM)
    return pl.pallas_call(
        kernel,
        out_shape=jax.ShapeDtypeStruct((NX, 2 * part, columns), f32),
        in_specs=[pl.BlockSpec(memory_space=pl.ANY)] * (count + 3),
        out_specs=spec,
        scratch_shapes=[
            pltpu.VMEM((NX * block, 2 * half), bf16),
            pltpu.VMEM(w_mine.shape, bf16),
            pltpu.VMEM(w_other.shape, bf16),
            pltpu.VMEM(w_keyval.shape, bf16),
            pltpu.SemaphoreType.DMA((2 * NX * NZ + 3,)),
        ],
        compiler_params=pltpu.CompilerParams(vmem_limit_bytes=60 * 1024 * 1024),
        cost_estimate=pl.CostEstimate(
            flops=8 * NX * block * half * (columns + fresh),
            bytes_accessed=4 * NX * block * half + 8 * half * columns,
            transcendentals=0,
        ),
        name="project",
    )(*messages, w_mine, w_other, w_keyval)


def on_device(
    hidden, norm_gain, w_query, w_keyval, w_out, cache_keys, cache_values, cache_lengths, positions
):
    x, y, z, c = (lax.axis_index(a) for a in "xyzc")
    rows, steps, width = hidden.shape
    tokens = rows * steps
    half = width // 2
    head_cols = w_query.shape[1]
    keyval_cols = w_keyval.shape[2]

    def in_core_order(own, swapped, axis):
        return jnp.where(
            c == 0, jnp.stack([own, swapped], axis=axis), jnp.stack([swapped, own], axis=axis)
        )

    features = hidden.reshape(tokens, width).astype(f32)
    squares = jnp.sum(features * features, axis=-1)
    square_sums = squares + recv(squares, "y", 1) + recv(squares, "y", 2) + recv(squares, "y", 3)
    inverse = lax.rsqrt(square_sums / (width * NY) + norm_epsilon)
    normed = (features * inverse[:, None] * norm_gain.astype(f32)).astype(bf16)
    places = positions.astype(f32)[:, None] + jnp.arange(steps, dtype=f32)[None, :]
    angles = places.reshape(-1)[:, None] * rope_rates()
    cosine, sine = jnp.cos(angles), jnp.sin(angles)
    cosine = jnp.concatenate([cosine, cosine], axis=1)
    sine = jnp.concatenate([-sine, sine], axis=1)
    tables = (jnp.tile(cosine, (2, 1)), jnp.tile(sine, (2, 1)))
    messages, item_places, tables = gather_rows(
        jnp.concatenate([normed[:, :half], normed[:, half:]]), tables
    )
    cosine, sine = tables[0][:TOKENS], tables[1][:TOKENS]

    w_query, w_keyval, w_out, _ = lax.optimization_barrier(
        (w_query, w_keyval, w_out, messages[1])
    )
    w_query_other = recv(w_query, "c", 1)
    w_keyval = w_keyval.transpose(0, 2, 1).reshape(2 * keyval_cols, width)
    w_keyval = jnp.concatenate([w_keyval, recv(w_keyval, "c", 1)])
    w_out = jnp.concatenate([w_out, recv(w_out, "c", 1)])

    partial = project(messages, item_places, w_query, w_query_other, w_keyval)
    block = NZ * tokens

    def block_for(d):
        return lax.dynamic_index_in_dim(partial, (y + d - x + NX) % NX, 0, keepdims=False)

    summed = block_for(0)
    for d in (1, 2, 3):
        summed = summed + recv(block_for(d), "y", -d)
    summed = summed.astype(bf16)
    part = summed.shape[0] // 2
    own, swapped = summed[:part], recv(summed[part:], "c", 1)

    def queries_of(a):
        return a[:block].reshape(NZ, tokens, head_cols)

    def keyvals_of(a):
        a = jnp.concatenate([a[block:, :block], a[block:, block:]])
        return a.T.reshape(NZ, tokens, 2 * keyval_cols)

    back = (NZ - z) % NZ
    q = roll_to(in_core_order(queries_of(own), queries_of(swapped), 1), back)
    kv = roll_to(in_core_order(keyvals_of(own), keyvals_of(swapped), 1), back)
    places_out = 2 * block // TOKENS
    q = q.reshape(places_out, TOKENS, head_cols // HD, HD).transpose(0, 2, 1, 3)
    q = q.reshape(places_out, -1, HD)
    kv = kv.reshape(places_out, 1, -1)
    arrived = lax.all_to_all(
        jnp.concatenate([q, kv], axis=1), ("x", "z", "c"), split_axis=0, concat_axis=0, tiled=True
    )
    q_rows = q.shape[1]
    queries = arrived[:, :q_rows].reshape(-1, HD)
    keyvals = arrived[:, q_rows].reshape(places_out, TOKENS, 2, keyval_cols)
    keyvals = keyvals.transpose(2, 1, 0, 3).reshape(2, TOKENS, KVH, HD)
    fresh_keys = keyvals[0].astype(f32)
    turned_keys = (
        fresh_keys * cosine[:, None] + jnp.roll(fresh_keys, HALF, axis=-1) * sine[:, None]
    ).astype(bf16)
    new = jnp.stack([turned_keys, keyvals[1]]).reshape(2, TOKENS, KVH * HD)
    padded = jnp.pad(new, ((0, 0), (0, 16 - TOKENS), (0, 0)))
    attended = attend(
        queries,
        *tables,
        cache_keys,
        cache_values,
        padded,
        cache_lengths,
    )
    returned = lax.all_to_all(
        attended.reshape(places_out, -1, HD), ("x", "z", "c"), split_axis=0, concat_axis=0, tiled=True
    )
    returned = returned.reshape(places_out, head_cols // HD, TOKENS, HD).transpose(0, 2, 1, 3)
    returned = roll_to(returned.reshape(NZ, NC, tokens, head_cols), z)
    kept = lax.dynamic_index_in_dim(returned, c, 1, keepdims=False)
    got = recv(lax.dynamic_index_in_dim(returned, 1 - c, 1, keepdims=False), "c", 1)
    returned = jnp.concatenate([kept, got], axis=2).reshape(block, 2 * head_cols)
    line = jnp.stack([returned] + [recv(returned, "y", d) for d in (1, 2, 3)])
    new_keyvals = new.reshape(2, TOKENS // steps, steps, KVH * HD)
    line, new_keyvals = lax.optimization_barrier((line, new_keyvals))
    left = jnp.concatenate(
        [
            lax.dynamic_index_in_dim(line, (x + i - y + NX) % NX, 0, keepdims=False)
            for i in range(NX)
        ]
    )
    branch = scatter_rows(dot(left, w_out), tokens)
    return branch.reshape(rows, steps, width), new_keyvals


def solution(mesh):
    fine = Mesh(mesh.devices.reshape(NY, NX, NZ, NC), ("y", "x", "z", "c"))
    gy = ("x", "z", "c")
    everywhere = ("y", "x", "z", "c")
    return jax.shard_map(
        on_device,
        mesh=fine,
        in_specs=(
            P(gy, None, "y"),
            P("y"),
            P("y", gy),
            P(None, "y", gy),
            P(gy, "y"),
            P(everywhere, None, None),
            P(everywhere, None, None),
            P(everywhere),
            P(everywhere),
        ),
        out_specs=(P(gy, None, "y"), P(None, everywhere, None, None)),
        check_vma=False,
    )
```

```python
import math

import jax
import jax.numpy as jnp
from jax import lax
from jax.experimental import pallas as pl
from jax.experimental.pallas import tpu as pltpu
from jax.sharding import Mesh
from jax.sharding import PartitionSpec as P

HQ = 128
KVH = 8
HD = 128
HALF = HD // 2
TOKENS = 4
NX, NY, NZ, NC = 4, 4, 8, 2
f32 = jnp.float32
bf16 = jnp.bfloat16

norm_epsilon = 1e-05


def rope_rates():
    index = jnp.arange(HD // 2, dtype=jnp.float32)
    rates = 1.0 / jnp.power(500000.0, 2.0 * index / HD)
    wavelength = 2.0 * math.pi / rates
    smooth = (8192.0 / wavelength - 1.0) / 3.0
    blended = (1.0 - smooth) * rates / 8.0 + smooth * rates
    return jnp.where(
        wavelength > 8192.0, rates / 8.0, jnp.where(wavelength < 2048.0, rates, blended)
    )


def recv(block, axis, distance):
    size = lax.axis_size(axis)
    return lax.ppermute(block, axis, [((i + distance) % size, i) for i in range(size)])


def roll_to(blocks, start):
    return lax.dynamic_slice_in_dim(
        jnp.concatenate([blocks, blocks], axis=0), start, blocks.shape[0], 0
    )


def dot(a, b):
    return jnp.dot(a, b, preferred_element_type=f32)


HEADS_AT_ONCE = 2


def attention_kernel(lengths, q, cosine, sine, k_old, v_old, k_new, v_new, out):
    rows = q.shape[0] // HEADS_AT_ONCE
    slots = k_old.shape[1]
    repeats = rows // cosine.shape[0]
    cosines = jnp.concatenate([cosine[...]] * repeats)
    sines = jnp.concatenate([sine[...]] * repeats)
    contract_last = (((1,), (1,)), ((), ()))
    score_scale = HD ** (-0.5)
    token = lax.broadcasted_iota(jnp.int32, (rows, 1), 0) % TOKENS
    first = token < 2
    slot = lax.broadcasted_iota(jnp.int32, (rows, slots), 1)
    valid = slot < jnp.where(first, lengths[0], lengths[1])
    for head in range(HEADS_AT_ONCE):
        mine = slice(head * rows, (head + 1) * rows)
        lanes = slice(head * HD, (head + 1) * HD)
        queries = q[mine, :].astype(f32)
        turned = (queries * cosines + pltpu.roll(queries, HALF, 1) * sines).astype(bf16)

        def scores(keys):
            return lax.dot_general(turned, keys, contract_last, preferred_element_type=f32)

        old = jnp.where(first, scores(k_old[0, :, lanes]), scores(k_old[1, :, lanes]))
        old = jnp.where(valid, old * score_scale, -1e30)
        fresh = scores(k_new[:, lanes]) * score_scale
        other = lax.broadcasted_iota(jnp.int32, fresh.shape, 1)
        keep = (other // 2 == token // 2) & (other <= token)
        fresh = jnp.where(keep, fresh, -1e30)
        highest = jnp.maximum(
            jnp.max(old, axis=1, keepdims=True), jnp.max(fresh, axis=1, keepdims=True)
        )
        old = jnp.exp(old - highest)
        fresh = jnp.exp(fresh - highest)
        denom = jnp.sum(old, axis=1, keepdims=True) + jnp.sum(fresh, axis=1, keepdims=True)
        mixed = (
            dot(jnp.where(first, old, 0.0).astype(bf16), v_old[0, :, lanes])
            + dot(jnp.where(first, 0.0, old).astype(bf16), v_old[1, :, lanes])
            + dot(fresh.astype(bf16), v_new[:, lanes])
        )
        out[mine, :] = (mixed / denom).astype(bf16)


def attend(q, cosine, sine, cache_keys, cache_values, new, lengths):
    step_rows = q.shape[0] // KVH * HEADS_AT_ONCE
    step_cols = HD * HEADS_AT_ONCE
    slots = cache_keys.shape[1]
    fresh_rows = new.shape[1]
    return pl.pallas_call(
        attention_kernel,
        out_shape=jax.ShapeDtypeStruct(q.shape, bf16),
        grid_spec=pltpu.PrefetchScalarGridSpec(
            num_scalar_prefetch=1,
            grid=(KVH // HEADS_AT_ONCE,),
            in_specs=[
                pl.BlockSpec((step_rows, HD), lambda g, n: (g, 0)),
                pl.BlockSpec(cosine.shape, lambda g, n: (0, 0)),
                pl.BlockSpec(sine.shape, lambda g, n: (0, 0)),
                pl.BlockSpec((2, slots, step_cols), lambda g, n: (0, 0, g)),
                pl.BlockSpec((2, slots, step_cols), lambda g, n: (0, 0, g)),
                pl.BlockSpec((None, fresh_rows, step_cols), lambda g, n: (0, 0, g)),
                pl.BlockSpec((None, fresh_rows, step_cols), lambda g, n: (1, 0, g)),
            ],
            out_specs=pl.BlockSpec((step_rows, HD), lambda g, n: (g, 0)),
        ),
        compiler_params=pltpu.CompilerParams(vmem_limit_bytes=56 * 1024 * 1024),
        cost_estimate=pl.CostEstimate(
            flops=8 * q.shape[0] * slots * HD,
            bytes_accessed=8 * slots * KVH * HD,
            transcendentals=q.shape[0] * slots,
        ),
        name="attention",
    )(lengths, q, cosine, sine, cache_keys, cache_values, new, new)


LOWER, UPPER = 0, 1
DIRECTIONS = {"z+": ("z", 1), "z-": ("z", -1), "x+": ("x", 1), "x-": ("x", -1), "x2": ("x", 2)}


def tree_rounds():
    a, b = LOWER, UPPER
    return [
        {
            "z+": [(b, 0, 1), (a, 0, 1)],
            "z-": [(b, 0, 7), (a, 0, 7)],
            "x+": [(a, 1, 0), (b, 1, 0)],
            "x-": [(a, 3, 0), (b, 3, 0)],
            "x2": [(a, 2, 0)],
        },
        {
            "z+": [(b, 0, 2), (a, 0, 2), (a, 1, 1), (a, 3, 1), (a, 2, 1)],
            "z-": [(b, 0, 6), (a, 0, 6), (a, 1, 7), (a, 3, 7), (a, 2, 7)],
            "x+": [(b, 1, 1), (b, 1, 7)],
            "x-": [(b, 2, 0), (b, 3, 1), (b, 3, 7)],
        },
        {
            "z+": [(b, 0, 3), (a, 0, 3), (a, 1, 2), (a, 3, 2), (a, 2, 2)],
            "z-": [(b, 0, 5), (a, 0, 5), (a, 1, 6), (a, 3, 6), (a, 2, 6)],
            "x+": [(b, 2, 1), (b, 1, 2), (b, 1, 6)],
            "x-": [(b, 2, 7), (b, 3, 2), (b, 3, 6)],
        },
        {
            "z+": [(a, 0, 4), (a, 1, 3), (a, 3, 3), (a, 2, 3)],
            "z-": [(b, 0, 4), (a, 1, 5), (a, 3, 5), (a, 2, 5)],
            "x+": [(b, 2, 2), (b, 1, 3), (b, 1, 5)],
            "x-": [(b, 2, 6), (b, 3, 3), (b, 3, 5)],
        },
        {
            "z+": [(a, 1, 4), (a, 2, 4)],
            "z-": [(a, 3, 4)],
            "x+": [(b, 2, 3), (b, 1, 4)],
            "x-": [(b, 2, 5), (b, 3, 4)],
            "x2": [(b, 2, 4)],
        },
    ]


def seen_from(item, direction):
    which, dx, dz = item
    axis, sign = DIRECTIONS[direction]
    return (which, (dx - sign) % NX, dz) if axis == "x" else (which, dx, (dz - sign) % NZ)


def gather_rows(piece):
    rows = piece.shape[0] // 2
    messages = [piece]
    places = {(LOWER, 0, 0): (0, 0), (UPPER, 0, 0): (0, rows)}
    for exchange in tree_rounds():
        got = []
        for direction, items in exchange.items():
            held = [places[seen_from(item, direction)] for item in items]
            runs = []
            for message, row in held:
                if runs and runs[-1][0] == message and runs[-1][2] == row:
                    runs[-1][2] += rows
                else:
                    runs.append([message, row, row + rows])
            parts = [messages[m][lo:hi] for m, lo, hi in runs]
            got.append((recv(jnp.concatenate(parts), *DIRECTIONS[direction]), items))
        for message, items in got:
            for k, item in enumerate(items):
                places[item] = (len(messages), k * rows)
            messages.append(message)
    return messages, places


def sums(product, messages, wanted, rows, half):
    used = sorted({m for items in wanted for _, found in items for m, _ in found})
    count = sum(len(items) for items in wanted)

    def kernel(*refs):
        terms, sources = refs[0], dict(zip(used, refs[1 : 1 + len(used)]))
        outs, held, sems = refs[1 + len(used) : -2], refs[-2], refs[-1]
        copies = []
        for items in wanted:
            for (which, dx, dz), _ in items:
                n = len(copies)
                copies.append(
                    pltpu.make_async_copy(
                        terms.at[pl.ds((dx * NZ + dz) * rows, rows), pl.ds(which * half, half)],
                        held.at[n],
                        sems.at[n],
                    )
                )
                copies[-1].start()
        n = 0
        for out, items in zip(outs, wanted):
            for k, (_, found) in enumerate(items):
                copies[n].wait()
                total = held[n]
                for m, row in found:
                    total = total + sources[m][row : row + rows, :].astype(f32)
                out[k * rows : (k + 1) * rows, :] = total.astype(bf16)
                n += 1

    spec = pl.BlockSpec(memory_space=pltpu.VMEM)
    shapes = [jax.ShapeDtypeStruct((len(items) * rows, half), bf16) for items in wanted]
    return pl.pallas_call(
        kernel,
        out_shape=shapes,
        in_specs=[pl.BlockSpec(memory_space=pl.ANY)] + [spec] * len(used),
        out_specs=[spec] * len(shapes),
        scratch_shapes=[
            pltpu.VMEM((count, rows, half), f32),
            pltpu.SemaphoreType.DMA((count,)),
        ],
        compiler_params=pltpu.CompilerParams(vmem_limit_bytes=16 * 1024 * 1024),
        cost_estimate=pl.CostEstimate(
            flops=2 * count * rows * half, bytes_accessed=10 * count * rows * half, transcendentals=0
        ),
        name="sums",
    )(product, *[messages[m] for m in used])


def scatter_rows(product, rows):
    half = product.shape[1] // 2
    messages, found = [], {}
    for exchange in reversed(tree_rounds()):
        wanted = [[(item, found.get(item, [])) for item in items] for items in exchange.values()]
        sent = sums(product, messages, wanted, rows, half)
        got = [
            recv(message, DIRECTIONS[direction][0], -DIRECTIONS[direction][1])
            for direction, message in zip(exchange, sent)
        ]
        got = lax.optimization_barrier(got)
        for message, (direction, items) in zip(got, exchange.items()):
            for k, item in enumerate(items):
                found.setdefault(seen_from(item, direction), []).append((len(messages), k * rows))
            messages.append(message)
    own = [[(item, found[item])] for item in ((LOWER, 0, 0), (UPPER, 0, 0))]
    return jnp.concatenate(sums(product, messages, own, rows, half), axis=1)


def project(messages, places, w_mine, w_other, w_keyval):
    rows, half = messages[0].shape[0] // 2, messages[0].shape[1]
    block = rows * NZ
    columns = w_mine.shape[1]
    fresh = w_keyval.shape[0] // 2
    part = block + fresh // 2
    count = len(messages)
    together = 2

    def kernel(*refs):
        sources, (mine, other, keyval, out, held) = refs[:count], refs[count:]
        for dx in range(NX):
            for dz in range(NZ):
                for which in (LOWER, UPPER):
                    message, row = places[(which, dx, dz)]
                    to = dx * block + dz * rows
                    held[to : to + rows, which * half : (which + 1) * half] = sources[message][
                        row : row + rows, :
                    ]

        @pl.loop(0, NX // together)
        def _(step):
            size = together * block
            features = held[pl.ds(pl.multiple_of(step * size, size), size), :]
            q_mine = dot(features, mine[...])
            q_other = dot(features, other[...])
            kv = lax.dot_general(
                keyval[...], features, (((1,), (1,)), ((), ())), preferred_element_type=f32
            )
            for k in range(together):
                dx = step * together + k
                out[dx, :block, :] = q_mine[k * block : (k + 1) * block]
                out[dx, part : part + block, :] = q_other[k * block : (k + 1) * block]
                for core in range(NC):
                    top = core * part + block
                    for side in range(2):
                        first = core * fresh + side * fresh // 2
                        out[dx, top : top + fresh // 2, side * block : (side + 1) * block] = kv[
                            first : first + fresh // 2, k * block : (k + 1) * block
                        ]

    spec = pl.BlockSpec(memory_space=pltpu.VMEM)
    return pl.pallas_call(
        kernel,
        out_shape=jax.ShapeDtypeStruct((NX, 2 * part, columns), f32),
        in_specs=[spec] * (count + 3),
        out_specs=spec,
        scratch_shapes=[pltpu.VMEM((NX * block, 2 * half), bf16)],
        compiler_params=pltpu.CompilerParams(vmem_limit_bytes=32 * 1024 * 1024),
        cost_estimate=pl.CostEstimate(
            flops=8 * NX * block * half * (columns + fresh),
            bytes_accessed=4 * NX * block * half + 8 * half * columns,
            transcendentals=0,
        ),
        name="project",
    )(*messages, w_mine, w_other, w_keyval)


def on_device(
    hidden, norm_gain, w_query, w_keyval, w_out, cache_keys, cache_values, cache_lengths, positions
):
    x, y, z, c = (lax.axis_index(a) for a in "xyzc")
    rows, steps, width = hidden.shape
    tokens = rows * steps
    half = width // 2
    head_cols = w_query.shape[1]
    keyval_cols = w_keyval.shape[2]

    def in_core_order(own, swapped, axis):
        return jnp.where(
            c == 0, jnp.stack([own, swapped], axis=axis), jnp.stack([swapped, own], axis=axis)
        )

    features = hidden.reshape(tokens, width).astype(f32)
    squares = jnp.sum(features * features, axis=-1)
    square_sums = squares + recv(squares, "y", 1) + recv(squares, "y", 2) + recv(squares, "y", 3)
    inverse = lax.rsqrt(square_sums / (width * NY) + norm_epsilon)
    normed = (features * inverse[:, None] * norm_gain.astype(f32)).astype(bf16)
    messages, item_places = gather_rows(jnp.concatenate([normed[:, :half], normed[:, half:]]))

    w_query, w_keyval, w_out, _ = lax.optimization_barrier(
        (w_query, w_keyval, w_out, messages[1])
    )
    w_query_other = recv(w_query, "c", 1)
    w_keyval = w_keyval.transpose(0, 2, 1).reshape(2 * keyval_cols, width)
    w_keyval = jnp.concatenate([w_keyval, recv(w_keyval, "c", 1)])
    w_out = jnp.concatenate([w_out, recv(w_out, "c", 1)])

    places = positions.astype(f32)[:, None] + jnp.arange(steps, dtype=f32)[None, :]
    angles = places.reshape(-1)[:, None] * rope_rates()
    cosine, sine = jnp.cos(angles), jnp.sin(angles)
    cosine = jnp.concatenate([cosine, cosine], axis=1)
    sine = jnp.concatenate([-sine, sine], axis=1)

    partial = project(messages, item_places, w_query, w_query_other, w_keyval)
    block = NZ * tokens

    def block_for(d):
        return lax.dynamic_index_in_dim(partial, (y + d - x + NX) % NX, 0, keepdims=False)

    summed = block_for(0)
    for d in (1, 2, 3):
        summed = summed + recv(block_for(d), "y", -d)
    summed = summed.astype(bf16)
    part = summed.shape[0] // 2
    own, swapped = summed[:part], recv(summed[part:], "c", 1)

    def queries_of(a):
        return a[:block].reshape(NZ, tokens, head_cols)

    def keyvals_of(a):
        a = jnp.concatenate([a[block:, :block], a[block:, block:]])
        return a.T.reshape(NZ, tokens, 2 * keyval_cols)

    back = (NZ - z) % NZ
    q = roll_to(in_core_order(queries_of(own), queries_of(swapped), 1), back)
    kv = roll_to(in_core_order(keyvals_of(own), keyvals_of(swapped), 1), back)
    places_out = 2 * block // TOKENS
    q = q.reshape(places_out, TOKENS, head_cols // HD, HD).transpose(0, 2, 1, 3)
    q = q.reshape(places_out, -1, HD)
    kv = kv.reshape(places_out, 1, -1)
    arrived = lax.all_to_all(
        jnp.concatenate([q, kv], axis=1), ("x", "z", "c"), split_axis=0, concat_axis=0, tiled=True
    )
    q_rows = q.shape[1]
    queries = arrived[:, :q_rows].reshape(-1, HD)
    keyvals = arrived[:, q_rows].reshape(places_out, TOKENS, 2, keyval_cols)
    keyvals = keyvals.transpose(2, 1, 0, 3).reshape(2, TOKENS, KVH, HD)
    fresh_keys = keyvals[0].astype(f32)
    turned_keys = (
        fresh_keys * cosine[:, None] + jnp.roll(fresh_keys, HALF, axis=-1) * sine[:, None]
    ).astype(bf16)
    new = jnp.stack([turned_keys, keyvals[1]]).reshape(2, TOKENS, KVH * HD)
    padded = jnp.pad(new, ((0, 0), (0, 16 - TOKENS), (0, 0)))
    attended = attend(
        queries,
        jnp.tile(cosine, (2, 1)),
        jnp.tile(sine, (2, 1)),
        cache_keys,
        cache_values,
        padded,
        cache_lengths,
    )
    returned = lax.all_to_all(
        attended.reshape(places_out, -1, HD), ("x", "z", "c"), split_axis=0, concat_axis=0, tiled=True
    )
    returned = returned.reshape(places_out, head_cols // HD, TOKENS, HD).transpose(0, 2, 1, 3)
    returned = roll_to(returned.reshape(NZ, NC, tokens, head_cols), z)
    kept = lax.dynamic_index_in_dim(returned, c, 1, keepdims=False)
    got = recv(lax.dynamic_index_in_dim(returned, 1 - c, 1, keepdims=False), "c", 1)
    returned = jnp.concatenate([kept, got], axis=2).reshape(block, 2 * head_cols)
    line = jnp.stack([returned] + [recv(returned, "y", d) for d in (1, 2, 3)])
    new_keyvals = new.reshape(2, TOKENS // steps, steps, KVH * HD)
    line, new_keyvals = lax.optimization_barrier((line, new_keyvals))
    left = jnp.concatenate(
        [
            lax.dynamic_index_in_dim(line, (x + i - y + NX) % NX, 0, keepdims=False)
            for i in range(NX)
        ]
    )
    branch = scatter_rows(dot(left, w_out), tokens)
    return branch.reshape(rows, steps, width), new_keyvals


def solution(mesh):
    fine = Mesh(mesh.devices.reshape(NY, NX, NZ, NC), ("y", "x", "z", "c"))
    gy = ("x", "z", "c")
    everywhere = ("y", "x", "z", "c")
    return jax.shard_map(
        on_device,
        mesh=fine,
        in_specs=(
            P(gy, None, "y"),
            P("y"),
            P("y", gy),
            P(None, "y", gy),
            P(gy, "y"),
            P(everywhere, None, None),
            P(everywhere, None, None),
            P(everywhere),
            P(everywhere),
        ),
        out_specs=(P(gy, None, "y"), P(None, everywhere, None, None)),
        check_vma=False,
    )
```

```python
import math

import jax
import jax.numpy as jnp
from jax import lax
from jax.experimental import pallas as pl
from jax.experimental.pallas import tpu as pltpu
from jax.sharding import Mesh
from jax.sharding import PartitionSpec as P

HQ = 128
KVH = 8
HD = 128
HALF = HD // 2
TOKENS = 4
NX, NY, NZ, NC = 4, 4, 8, 2
f32 = jnp.float32
bf16 = jnp.bfloat16

norm_epsilon = 1e-05


def rope_rates():
    index = jnp.arange(HD // 2, dtype=jnp.float32)
    rates = 1.0 / jnp.power(500000.0, 2.0 * index / HD)
    wavelength = 2.0 * math.pi / rates
    smooth = (8192.0 / wavelength - 1.0) / 3.0
    blended = (1.0 - smooth) * rates / 8.0 + smooth * rates
    return jnp.where(
        wavelength > 8192.0, rates / 8.0, jnp.where(wavelength < 2048.0, rates, blended)
    )


def recv(block, axis, distance):
    size = lax.axis_size(axis)
    return lax.ppermute(block, axis, [((i + distance) % size, i) for i in range(size)])


def roll_to(blocks, start):
    return lax.dynamic_slice_in_dim(
        jnp.concatenate([blocks, blocks], axis=0), start, blocks.shape[0], 0
    )


def dot(a, b):
    return jnp.dot(a, b, preferred_element_type=f32)


HEADS_AT_ONCE = 2


def attention_kernel(lengths, q, cosine, sine, k_old, v_old, k_new, v_new, out):
    rows = q.shape[0] // HEADS_AT_ONCE
    slots = k_old.shape[1]
    repeats = rows // cosine.shape[0]
    cosines = jnp.concatenate([cosine[...]] * repeats)
    sines = jnp.concatenate([sine[...]] * repeats)
    contract_last = (((1,), (1,)), ((), ()))
    score_scale = HD ** (-0.5)
    token = lax.broadcasted_iota(jnp.int32, (rows, 1), 0) % TOKENS
    first = token < 2
    slot = lax.broadcasted_iota(jnp.int32, (rows, slots), 1)
    valid = slot < jnp.where(first, lengths[0], lengths[1])
    for head in range(HEADS_AT_ONCE):
        mine = slice(head * rows, (head + 1) * rows)
        lanes = slice(head * HD, (head + 1) * HD)
        queries = q[mine, :].astype(f32)
        turned = (queries * cosines + pltpu.roll(queries, HALF, 1) * sines).astype(bf16)

        def scores(keys):
            return lax.dot_general(turned, keys, contract_last, preferred_element_type=f32)

        old = jnp.where(first, scores(k_old[0, :, lanes]), scores(k_old[1, :, lanes]))
        old = jnp.where(valid, old * score_scale, -1e30)
        fresh = scores(k_new[:, lanes]) * score_scale
        other = lax.broadcasted_iota(jnp.int32, fresh.shape, 1)
        keep = (other // 2 == token // 2) & (other <= token)
        fresh = jnp.where(keep, fresh, -1e30)
        highest = jnp.maximum(
            jnp.max(old, axis=1, keepdims=True), jnp.max(fresh, axis=1, keepdims=True)
        )
        old = jnp.exp(old - highest)
        fresh = jnp.exp(fresh - highest)
        denom = jnp.sum(old, axis=1, keepdims=True) + jnp.sum(fresh, axis=1, keepdims=True)
        mixed = (
            dot(jnp.where(first, old, 0.0).astype(bf16), v_old[0, :, lanes])
            + dot(jnp.where(first, 0.0, old).astype(bf16), v_old[1, :, lanes])
            + dot(fresh.astype(bf16), v_new[:, lanes])
        )
        out[mine, :] = (mixed / denom).astype(bf16)


def attend(q, cosine, sine, cache_keys, cache_values, new, lengths):
    step_rows = q.shape[0] // KVH * HEADS_AT_ONCE
    step_cols = HD * HEADS_AT_ONCE
    slots = cache_keys.shape[1]
    fresh_rows = new.shape[1]
    return pl.pallas_call(
        attention_kernel,
        out_shape=jax.ShapeDtypeStruct(q.shape, bf16),
        grid_spec=pltpu.PrefetchScalarGridSpec(
            num_scalar_prefetch=1,
            grid=(KVH // HEADS_AT_ONCE,),
            in_specs=[
                pl.BlockSpec((step_rows, HD), lambda g, n: (g, 0)),
                pl.BlockSpec(cosine.shape, lambda g, n: (0, 0)),
                pl.BlockSpec(sine.shape, lambda g, n: (0, 0)),
                pl.BlockSpec((2, slots, step_cols), lambda g, n: (0, 0, g)),
                pl.BlockSpec((2, slots, step_cols), lambda g, n: (0, 0, g)),
                pl.BlockSpec((None, fresh_rows, step_cols), lambda g, n: (0, 0, g)),
                pl.BlockSpec((None, fresh_rows, step_cols), lambda g, n: (1, 0, g)),
            ],
            out_specs=pl.BlockSpec((step_rows, HD), lambda g, n: (g, 0)),
        ),
        compiler_params=pltpu.CompilerParams(vmem_limit_bytes=56 * 1024 * 1024),
        cost_estimate=pl.CostEstimate(
            flops=8 * q.shape[0] * slots * HD,
            bytes_accessed=8 * slots * KVH * HD,
            transcendentals=q.shape[0] * slots,
        ),
        name="attention",
    )(lengths, q, cosine, sine, cache_keys, cache_values, new, new)


LOWER, UPPER = 0, 1
DIRECTIONS = {"z+": ("z", 1), "z-": ("z", -1), "x+": ("x", 1), "x-": ("x", -1), "x2": ("x", 2)}


def tree_rounds():
    a, b = LOWER, UPPER
    return [
        {
            "z+": [(b, 0, 1), (a, 0, 1)],
            "z-": [(b, 0, 7), (a, 0, 7)],
            "x+": [(a, 1, 0), (b, 1, 0)],
            "x-": [(a, 3, 0), (b, 3, 0)],
            "x2": [(a, 2, 0)],
        },
        {
            "z+": [(b, 0, 2), (a, 0, 2), (a, 1, 1), (a, 3, 1), (a, 2, 1)],
            "z-": [(b, 0, 6), (a, 0, 6), (a, 1, 7), (a, 3, 7), (a, 2, 7)],
            "x+": [(b, 1, 1), (b, 1, 7)],
            "x-": [(b, 2, 0), (b, 3, 1), (b, 3, 7)],
        },
        {
            "z+": [(b, 0, 3), (a, 0, 3), (a, 1, 2), (a, 3, 2), (a, 2, 2)],
            "z-": [(b, 0, 5), (a, 0, 5), (a, 1, 6), (a, 3, 6), (a, 2, 6)],
            "x+": [(b, 2, 1), (b, 1, 2), (b, 1, 6)],
            "x-": [(b, 2, 7), (b, 3, 2), (b, 3, 6)],
        },
        {
            "z+": [(a, 0, 4), (a, 1, 3), (a, 3, 3), (a, 2, 3)],
            "z-": [(b, 0, 4), (a, 1, 5), (a, 3, 5), (a, 2, 5)],
            "x+": [(b, 2, 2), (b, 1, 3), (b, 1, 5)],
            "x-": [(b, 2, 6), (b, 3, 3), (b, 3, 5)],
        },
        {
            "z+": [(a, 1, 4), (a, 2, 4)],
            "z-": [(a, 3, 4)],
            "x+": [(b, 2, 3), (b, 1, 4)],
            "x-": [(b, 2, 5), (b, 3, 4)],
            "x2": [(b, 2, 4)],
        },
    ]


def seen_from(item, direction):
    which, dx, dz = item
    axis, sign = DIRECTIONS[direction]
    return (which, (dx - sign) % NX, dz) if axis == "x" else (which, dx, (dz - sign) % NZ)


def gather_rows(piece):
    rows = piece.shape[0] // 2
    messages = [piece]
    places = {(LOWER, 0, 0): (0, 0), (UPPER, 0, 0): (0, rows)}
    for exchange in tree_rounds():
        got = []
        for direction, items in exchange.items():
            held = [places[seen_from(item, direction)] for item in items]
            runs = []
            for message, row in held:
                if runs and runs[-1][0] == message and runs[-1][2] == row:
                    runs[-1][2] += rows
                else:
                    runs.append([message, row, row + rows])
            parts = [messages[m][lo:hi] for m, lo, hi in runs]
            got.append((recv(jnp.concatenate(parts), *DIRECTIONS[direction]), items))
        for message, items in got:
            for k, item in enumerate(items):
                places[item] = (len(messages), k * rows)
            messages.append(message)
    return messages, places


def sums(product, messages, wanted, rows, half):
    used = sorted({m for items in wanted for _, found in items for m, _ in found})
    count = sum(len(items) for items in wanted)

    def kernel(*refs):
        terms, sources = refs[0], dict(zip(used, refs[1 : 1 + len(used)]))
        outs, held, sems = refs[1 + len(used) : -2], refs[-2], refs[-1]
        copies = []
        for items in wanted:
            for (which, dx, dz), _ in items:
                n = len(copies)
                copies.append(
                    pltpu.make_async_copy(
                        terms.at[pl.ds((dx * NZ + dz) * rows, rows), pl.ds(which * half, half)],
                        held.at[n],
                        sems.at[n],
                    )
                )
                copies[-1].start()
        n = 0
        for out, items in zip(outs, wanted):
            for k, (_, found) in enumerate(items):
                copies[n].wait()
                total = held[n]
                for m, row in found:
                    total = total + sources[m][row : row + rows, :].astype(f32)
                out[k * rows : (k + 1) * rows, :] = total.astype(bf16)
                n += 1

    spec = pl.BlockSpec(memory_space=pltpu.VMEM)
    shapes = [jax.ShapeDtypeStruct((len(items) * rows, half), bf16) for items in wanted]
    return pl.pallas_call(
        kernel,
        out_shape=shapes,
        in_specs=[pl.BlockSpec(memory_space=pl.ANY)] + [spec] * len(used),
        out_specs=[spec] * len(shapes),
        scratch_shapes=[
            pltpu.VMEM((count, rows, half), f32),
            pltpu.SemaphoreType.DMA((count,)),
        ],
        compiler_params=pltpu.CompilerParams(vmem_limit_bytes=16 * 1024 * 1024),
        cost_estimate=pl.CostEstimate(
            flops=2 * count * rows * half, bytes_accessed=10 * count * rows * half, transcendentals=0
        ),
        name="sums",
    )(product, *[messages[m] for m in used])


def scatter_rows(product, rows):
    half = product.shape[1] // 2
    messages, found = [], {}
    for exchange in reversed(tree_rounds()):
        wanted = [[(item, found.get(item, [])) for item in items] for items in exchange.values()]
        sent = sums(product, messages, wanted, rows, half)
        got = [
            recv(message, DIRECTIONS[direction][0], -DIRECTIONS[direction][1])
            for direction, message in zip(exchange, sent)
        ]
        got = lax.optimization_barrier(got)
        for message, (direction, items) in zip(got, exchange.items()):
            for k, item in enumerate(items):
                found.setdefault(seen_from(item, direction), []).append((len(messages), k * rows))
            messages.append(message)
    own = [[(item, found[item])] for item in ((LOWER, 0, 0), (UPPER, 0, 0))]
    return jnp.concatenate(sums(product, messages, own, rows, half), axis=1)


def project(messages, places, weights, distances, before=None):
    rows, half = messages[0].shape[0] // 2, messages[0].shape[1]
    block = rows * NZ
    columns = weights[0].shape[1]
    fresh = weights[2].shape[0] // 2
    part = block + fresh // 2
    taken = rows * len(distances)
    items = [(which, dx, dz) for dx in range(NX) for dz in distances for which in (LOWER, UPPER)]
    used = sorted({places[item][0] for item in items})
    runs = []
    for k, dz in enumerate(distances):
        if runs and runs[-1][1] + runs[-1][2] == dz * rows:
            runs[-1][2] += rows
        else:
            runs.append([k * rows, dz * rows, rows])
    together = 2
    shape = jax.ShapeDtypeStruct((NX, 2 * part, columns), f32)

    def kernel(*refs):
        sources, refs = dict(zip(used, refs)), refs[len(used) :]
        given, refs = refs[:3], refs[3:]
        out, held, mine, other, keyval, sems = refs[-6:]
        copies = []

        def fetch(source, target):
            copies.append(pltpu.make_async_copy(source, target, sems.at[len(copies)]))
            copies[-1].start()

        for source, target in zip(given, (mine, other, keyval)):
            fetch(source, target)
        for which, dx, dz in items:
            message, row = places[(which, dx, dz)]
            fetch(
                sources[message].at[pl.ds(row, rows), :],
                held.at[
                    pl.ds(dx * taken + distances.index(dz) * rows, rows),
                    pl.ds(which * half, half),
                ],
            )
        if before is not None:
            out[...] = refs[0][...]
        for copy in copies:
            copy.wait()

        @pl.loop(0, NX // together)
        def _(step):
            size = together * taken
            features = held[pl.ds(pl.multiple_of(step * size, size), size), :]
            q_mine = dot(features, mine[...])
            q_other = dot(features, other[...])
            for k in range(together):
                dx = step * together + k
                for at, to, size in runs:
                    at = k * taken + at
                    out[dx, to : to + size, :] = q_mine[at : at + size]
                    out[dx, part + to : part + to + size, :] = q_other[at : at + size]
                    kv = lax.dot_general(
                        keyval[...],
                        features[at : at + size],
                        (((1,), (1,)), ((), ())),
                        preferred_element_type=f32,
                    )
                    for core in range(NC):
                        top = core * part + block
                        for side in range(2):
                            first = core * fresh + side * fresh // 2
                            lane = side * block + to
                            out[dx, top : top + fresh // 2, lane : lane + size] = kv[
                                first : first + fresh // 2
                            ]

    anywhere = pl.BlockSpec(memory_space=pl.ANY)
    inside = pl.BlockSpec(memory_space=pltpu.VMEM)
    operands = [messages[m] for m in used] + list(weights)
    in_specs = [anywhere] * len(operands)
    if before is not None:
        operands.append(before)
        in_specs.append(inside)
    return pl.pallas_call(
        kernel,
        out_shape=shape,
        in_specs=in_specs,
        out_specs=inside,
        scratch_shapes=[
            pltpu.VMEM((NX * taken, 2 * half), bf16),
            *[pltpu.VMEM(w.shape, bf16) for w in weights],
            pltpu.SemaphoreType.DMA((len(items) + 3,)),
        ],
        compiler_params=pltpu.CompilerParams(vmem_limit_bytes=60 * 1024 * 1024),
        cost_estimate=pl.CostEstimate(
            flops=8 * NX * taken * half * (columns + fresh),
            bytes_accessed=4 * NX * taken * half + 8 * half * columns,
            transcendentals=0,
        ),
        name="project",
    )(*operands)


def on_device(
    hidden, norm_gain, w_query, w_keyval, w_out, cache_keys, cache_values, cache_lengths, positions
):
    x, y, z, c = (lax.axis_index(a) for a in "xyzc")
    rows, steps, width = hidden.shape
    tokens = rows * steps
    half = width // 2
    head_cols = w_query.shape[1]
    keyval_cols = w_keyval.shape[2]

    def in_core_order(own, swapped, axis):
        return jnp.where(
            c == 0, jnp.stack([own, swapped], axis=axis), jnp.stack([swapped, own], axis=axis)
        )

    features = hidden.reshape(tokens, width).astype(f32)
    squares = jnp.sum(features * features, axis=-1)
    square_sums = squares + recv(squares, "y", 1) + recv(squares, "y", 2) + recv(squares, "y", 3)
    inverse = lax.rsqrt(square_sums / (width * NY) + norm_epsilon)
    normed = (features * inverse[:, None] * norm_gain.astype(f32)).astype(bf16)
    messages, item_places = gather_rows(jnp.concatenate([normed[:, :half], normed[:, half:]]))

    w_query, w_keyval, w_out, _ = lax.optimization_barrier(
        (w_query, w_keyval, w_out, messages[1])
    )
    w_query_other = recv(w_query, "c", 1)
    w_keyval = w_keyval.transpose(0, 2, 1).reshape(2 * keyval_cols, width)
    w_keyval = jnp.concatenate([w_keyval, recv(w_keyval, "c", 1)])
    w_out = jnp.concatenate([w_out, recv(w_out, "c", 1)])

    places = positions.astype(f32)[:, None] + jnp.arange(steps, dtype=f32)[None, :]
    angles = places.reshape(-1)[:, None] * rope_rates()
    cosine, sine = jnp.cos(angles), jnp.sin(angles)
    cosine = jnp.concatenate([cosine, cosine], axis=1)
    sine = jnp.concatenate([-sine, sine], axis=1)

    weights = (w_query, w_query_other, w_keyval)
    partial = project(messages, item_places, weights, [0, 1, 2, 6, 7])
    partial = project(messages, item_places, weights, [3, 4, 5], partial)
    block = NZ * tokens

    def block_for(d):
        return lax.dynamic_index_in_dim(partial, (y + d - x + NX) % NX, 0, keepdims=False)

    summed = block_for(0)
    for d in (1, 2, 3):
        summed = summed + recv(block_for(d), "y", -d)
    summed = summed.astype(bf16)
    part = summed.shape[0] // 2
    own, swapped = summed[:part], recv(summed[part:], "c", 1)

    def queries_of(a):
        return a[:block].reshape(NZ, tokens, head_cols)

    def keyvals_of(a):
        a = jnp.concatenate([a[block:, :block], a[block:, block:]])
        return a.T.reshape(NZ, tokens, 2 * keyval_cols)

    back = (NZ - z) % NZ
    q = roll_to(in_core_order(queries_of(own), queries_of(swapped), 1), back)
    kv = roll_to(in_core_order(keyvals_of(own), keyvals_of(swapped), 1), back)
    places_out = 2 * block // TOKENS
    q = q.reshape(places_out, TOKENS, head_cols // HD, HD).transpose(0, 2, 1, 3)
    q = q.reshape(places_out, -1, HD)
    kv = kv.reshape(places_out, 1, -1)
    arrived = lax.all_to_all(
        jnp.concatenate([q, kv], axis=1), ("x", "z", "c"), split_axis=0, concat_axis=0, tiled=True
    )
    q_rows = q.shape[1]
    queries = arrived[:, :q_rows].reshape(-1, HD)
    keyvals = arrived[:, q_rows].reshape(places_out, TOKENS, 2, keyval_cols)
    keyvals = keyvals.transpose(2, 1, 0, 3).reshape(2, TOKENS, KVH, HD)
    fresh_keys = keyvals[0].astype(f32)
    turned_keys = (
        fresh_keys * cosine[:, None] + jnp.roll(fresh_keys, HALF, axis=-1) * sine[:, None]
    ).astype(bf16)
    new = jnp.stack([turned_keys, keyvals[1]]).reshape(2, TOKENS, KVH * HD)
    padded = jnp.pad(new, ((0, 0), (0, 16 - TOKENS), (0, 0)))
    attended = attend(
        queries,
        jnp.tile(cosine, (2, 1)),
        jnp.tile(sine, (2, 1)),
        cache_keys,
        cache_values,
        padded,
        cache_lengths,
    )
    returned = lax.all_to_all(
        attended.reshape(places_out, -1, HD), ("x", "z", "c"), split_axis=0, concat_axis=0, tiled=True
    )
    returned = returned.reshape(places_out, head_cols // HD, TOKENS, HD).transpose(0, 2, 1, 3)
    returned = roll_to(returned.reshape(NZ, NC, tokens, head_cols), z)
    kept = lax.dynamic_index_in_dim(returned, c, 1, keepdims=False)
    got = recv(lax.dynamic_index_in_dim(returned, 1 - c, 1, keepdims=False), "c", 1)
    returned = jnp.concatenate([kept, got], axis=2).reshape(block, 2 * head_cols)
    line = jnp.stack([returned] + [recv(returned, "y", d) for d in (1, 2, 3)])
    new_keyvals = new.reshape(2, TOKENS // steps, steps, KVH * HD)
    line, new_keyvals = lax.optimization_barrier((line, new_keyvals))
    left = jnp.concatenate(
        [
            lax.dynamic_index_in_dim(line, (x + i - y + NX) % NX, 0, keepdims=False)
            for i in range(NX)
        ]
    )
    branch = scatter_rows(dot(left, w_out), tokens)
    return branch.reshape(rows, steps, width), new_keyvals


def solution(mesh):
    fine = Mesh(mesh.devices.reshape(NY, NX, NZ, NC), ("y", "x", "z", "c"))
    gy = ("x", "z", "c")
    everywhere = ("y", "x", "z", "c")
    return jax.shard_map(
        on_device,
        mesh=fine,
        in_specs=(
            P(gy, None, "y"),
            P("y"),
            P("y", gy),
            P(None, "y", gy),
            P(gy, "y"),
            P(everywhere, None, None),
            P(everywhere, None, None),
            P(everywhere),
            P(everywhere),
        ),
        out_specs=(P(gy, None, "y"), P(None, everywhere, None, None)),
        check_vma=False,
    )
```

```python
import math

import jax
import jax.numpy as jnp
from jax import lax
from jax.experimental import pallas as pl
from jax.experimental.pallas import tpu as pltpu
from jax.sharding import Mesh
from jax.sharding import PartitionSpec as P

HQ = 128
KVH = 8
HD = 128
HALF = HD // 2
TOKENS = 4
NX, NY, NZ, NC = 4, 4, 8, 2
f32 = jnp.float32
bf16 = jnp.bfloat16

norm_epsilon = 1e-05


def rope_rates():
    index = jnp.arange(HD // 2, dtype=jnp.float32)
    rates = 1.0 / jnp.power(500000.0, 2.0 * index / HD)
    wavelength = 2.0 * math.pi / rates
    smooth = (8192.0 / wavelength - 1.0) / 3.0
    blended = (1.0 - smooth) * rates / 8.0 + smooth * rates
    return jnp.where(
        wavelength > 8192.0, rates / 8.0, jnp.where(wavelength < 2048.0, rates, blended)
    )


def recv(block, axis, distance):
    size = lax.axis_size(axis)
    return lax.ppermute(block, axis, [((i + distance) % size, i) for i in range(size)])


def roll_to(blocks, start):
    return lax.dynamic_slice_in_dim(
        jnp.concatenate([blocks, blocks], axis=0), start, blocks.shape[0], 0
    )


def dot(a, b):
    return jnp.dot(a, b, preferred_element_type=f32)


HEADS_AT_ONCE = 2


def attention_kernel(lengths, q, cosine, sine, k_old, v_old, k_new, v_new, out):
    rows = q.shape[0] // HEADS_AT_ONCE
    slots = k_old.shape[1]
    repeats = rows // cosine.shape[0]
    cosines = jnp.concatenate([cosine[...]] * repeats)
    sines = jnp.concatenate([sine[...]] * repeats)
    contract_last = (((1,), (1,)), ((), ()))
    score_scale = HD ** (-0.5)
    token = lax.broadcasted_iota(jnp.int32, (rows, 1), 0) % TOKENS
    first = token < 2
    slot = lax.broadcasted_iota(jnp.int32, (rows, slots), 1)
    valid = slot < jnp.where(first, lengths[0], lengths[1])
    for head in range(HEADS_AT_ONCE):
        mine = slice(head * rows, (head + 1) * rows)
        lanes = slice(head * HD, (head + 1) * HD)
        queries = q[mine, :].astype(f32)
        turned = (queries * cosines + pltpu.roll(queries, HALF, 1) * sines).astype(bf16)

        def scores(keys):
            return lax.dot_general(turned, keys, contract_last, preferred_element_type=f32)

        old = jnp.where(first, scores(k_old[0, :, lanes]), scores(k_old[1, :, lanes]))
        old = jnp.where(valid, old * score_scale, -1e30)
        fresh = scores(k_new[:, lanes]) * score_scale
        other = lax.broadcasted_iota(jnp.int32, fresh.shape, 1)
        keep = (other // 2 == token // 2) & (other <= token)
        fresh = jnp.where(keep, fresh, -1e30)
        highest = jnp.maximum(
            jnp.max(old, axis=1, keepdims=True), jnp.max(fresh, axis=1, keepdims=True)
        )
        old = jnp.exp(old - highest)
        fresh = jnp.exp(fresh - highest)
        denom = jnp.sum(old, axis=1, keepdims=True) + jnp.sum(fresh, axis=1, keepdims=True)
        mixed = (
            dot(jnp.where(first, old, 0.0).astype(bf16), v_old[0, :, lanes])
            + dot(jnp.where(first, 0.0, old).astype(bf16), v_old[1, :, lanes])
            + dot(fresh.astype(bf16), v_new[:, lanes])
        )
        out[mine, :] = (mixed / denom).astype(bf16)


def attend(q, cosine, sine, cache_keys, cache_values, new, lengths):
    step_rows = q.shape[0] // KVH * HEADS_AT_ONCE
    step_cols = HD * HEADS_AT_ONCE
    slots = cache_keys.shape[1]
    fresh_rows = new.shape[1]
    return pl.pallas_call(
        attention_kernel,
        out_shape=jax.ShapeDtypeStruct(q.shape, bf16),
        grid_spec=pltpu.PrefetchScalarGridSpec(
            num_scalar_prefetch=1,
            grid=(KVH // HEADS_AT_ONCE,),
            in_specs=[
                pl.BlockSpec((step_rows, HD), lambda g, n: (g, 0)),
                pl.BlockSpec(cosine.shape, lambda g, n: (0, 0)),
                pl.BlockSpec(sine.shape, lambda g, n: (0, 0)),
                pl.BlockSpec((2, slots, step_cols), lambda g, n: (0, 0, g)),
                pl.BlockSpec((2, slots, step_cols), lambda g, n: (0, 0, g)),
                pl.BlockSpec((None, fresh_rows, step_cols), lambda g, n: (0, 0, g)),
                pl.BlockSpec((None, fresh_rows, step_cols), lambda g, n: (1, 0, g)),
            ],
            out_specs=pl.BlockSpec((step_rows, HD), lambda g, n: (g, 0)),
        ),
        compiler_params=pltpu.CompilerParams(vmem_limit_bytes=56 * 1024 * 1024),
        cost_estimate=pl.CostEstimate(
            flops=8 * q.shape[0] * slots * HD,
            bytes_accessed=8 * slots * KVH * HD,
            transcendentals=q.shape[0] * slots,
        ),
        name="attention",
    )(lengths, q, cosine, sine, cache_keys, cache_values, new, new)


LOWER, UPPER = 0, 1
DIRECTIONS = {"z+": ("z", 1), "z-": ("z", -1), "x+": ("x", 1), "x-": ("x", -1), "x2": ("x", 2)}


def tree_rounds():
    a, b = LOWER, UPPER
    return [
        {
            "z+": [(b, 0, 1), (a, 0, 1)],
            "z-": [(b, 0, 7), (a, 0, 7)],
            "x+": [(a, 1, 0), (b, 1, 0)],
            "x-": [(a, 3, 0), (b, 3, 0)],
            "x2": [(a, 2, 0)],
        },
        {
            "z+": [(b, 0, 2), (a, 0, 2), (a, 1, 1), (a, 3, 1), (a, 2, 1)],
            "z-": [(b, 0, 6), (a, 0, 6), (a, 1, 7), (a, 3, 7), (a, 2, 7)],
            "x+": [(b, 1, 1), (b, 1, 7)],
            "x-": [(b, 2, 0), (b, 3, 1), (b, 3, 7)],
        },
        {
            "z+": [(b, 0, 3), (a, 0, 3), (a, 1, 2), (a, 3, 2), (a, 2, 2)],
            "z-": [(b, 0, 5), (a, 0, 5), (a, 1, 6), (a, 3, 6), (a, 2, 6)],
            "x+": [(b, 2, 1), (b, 1, 2), (b, 1, 6)],
            "x-": [(b, 2, 7), (b, 3, 2), (b, 3, 6)],
        },
        {
            "z+": [(a, 0, 4), (a, 1, 3), (a, 3, 3), (a, 2, 3)],
            "z-": [(b, 0, 4), (a, 1, 5), (a, 3, 5), (a, 2, 5)],
            "x+": [(b, 2, 2), (b, 1, 3), (b, 1, 5)],
            "x-": [(b, 2, 6), (b, 3, 3), (b, 3, 5)],
        },
        {
            "z+": [(a, 1, 4), (a, 2, 4)],
            "z-": [(a, 3, 4)],
            "x+": [(b, 2, 3), (b, 1, 4)],
            "x-": [(b, 2, 5), (b, 3, 4)],
            "x2": [(b, 2, 4)],
        },
    ]


def seen_from(item, direction):
    which, dx, dz = item
    axis, sign = DIRECTIONS[direction]
    return (which, (dx - sign) % NX, dz) if axis == "x" else (which, dx, (dz - sign) % NZ)


def gather_rows(piece):
    rows = piece.shape[0] // 2
    messages = [piece]
    places = {(LOWER, 0, 0): (0, 0), (UPPER, 0, 0): (0, rows)}
    for exchange in tree_rounds():
        got = []
        for direction, items in exchange.items():
            held = [places[seen_from(item, direction)] for item in items]
            runs = []
            for message, row in held:
                if runs and runs[-1][0] == message and runs[-1][2] == row:
                    runs[-1][2] += rows
                else:
                    runs.append([message, row, row + rows])
            parts = [messages[m][lo:hi] for m, lo, hi in runs]
            got.append((recv(jnp.concatenate(parts), *DIRECTIONS[direction]), items))
        for message, items in got:
            for k, item in enumerate(items):
                places[item] = (len(messages), k * rows)
            messages.append(message)
    return messages, places


def sums(product, messages, wanted, rows, half):
    used = sorted({m for items in wanted for _, found in items for m, _ in found})
    count = sum(len(items) for items in wanted)

    def kernel(*refs):
        terms, sources = refs[0], dict(zip(used, refs[1 : 1 + len(used)]))
        outs, held, sems = refs[1 + len(used) : -2], refs[-2], refs[-1]
        copies = []
        for items in wanted:
            for (which, dx, dz), _ in items:
                n = len(copies)
                copies.append(
                    pltpu.make_async_copy(
                        terms.at[pl.ds((dx * NZ + dz) * rows, rows), pl.ds(which * half, half)],
                        held.at[n],
                        sems.at[n],
                    )
                )
                copies[-1].start()
        n = 0
        for out, items in zip(outs, wanted):
            for k, (_, found) in enumerate(items):
                copies[n].wait()
                total = held[n]
                for m, row in found:
                    total = total + sources[m][row : row + rows, :].astype(f32)
                out[k * rows : (k + 1) * rows, :] = total.astype(bf16)
                n += 1

    spec = pl.BlockSpec(memory_space=pltpu.VMEM)
    shapes = [jax.ShapeDtypeStruct((len(items) * rows, half), bf16) for items in wanted]
    return pl.pallas_call(
        kernel,
        out_shape=shapes,
        in_specs=[pl.BlockSpec(memory_space=pl.ANY)] + [spec] * len(used),
        out_specs=[spec] * len(shapes),
        scratch_shapes=[
            pltpu.VMEM((count, rows, half), f32),
            pltpu.SemaphoreType.DMA((count,)),
        ],
        compiler_params=pltpu.CompilerParams(vmem_limit_bytes=16 * 1024 * 1024),
        cost_estimate=pl.CostEstimate(
            flops=2 * count * rows * half, bytes_accessed=10 * count * rows * half, transcendentals=0
        ),
        name="sums",
    )(product, *[messages[m] for m in used])


def scatter_rows(product, rows):
    half = product.shape[1] // 2
    messages, found = [], {}
    for exchange in reversed(tree_rounds()):
        wanted = [[(item, found.get(item, [])) for item in items] for items in exchange.values()]
        sent = sums(product, messages, wanted, rows, half)
        got = [
            recv(message, DIRECTIONS[direction][0], -DIRECTIONS[direction][1])
            for direction, message in zip(exchange, sent)
        ]
        got = lax.optimization_barrier(got)
        for message, (direction, items) in zip(got, exchange.items()):
            for k, item in enumerate(items):
                found.setdefault(seen_from(item, direction), []).append((len(messages), k * rows))
            messages.append(message)
    own = [[(item, found[item])] for item in ((LOWER, 0, 0), (UPPER, 0, 0))]
    return jnp.concatenate(sums(product, messages, own, rows, half), axis=1)


def project(messages, places, w_mine, w_other, w_keyval):
    rows, half = messages[0].shape[0] // 2, messages[0].shape[1]
    block = rows * NZ
    columns = w_mine.shape[1]
    fresh = w_keyval.shape[0] // 2
    part = block + fresh // 2
    count = len(messages)
    together = 1

    def kernel(*refs):
        sources, (mine, other, keyval, out, held) = refs[:count], refs[count:]
        for dx in range(NX):
            for dz in range(NZ):
                for which in (LOWER, UPPER):
                    message, row = places[(which, dx, dz)]
                    to = dx * block + dz * rows
                    held[to : to + rows, which * half : (which + 1) * half] = sources[message][
                        row : row + rows, :
                    ]

        @pl.loop(0, NX // together)
        def _(step):
            size = together * block
            features = held[pl.ds(pl.multiple_of(step * size, size), size), :]
            q_mine = dot(features, mine[...])
            q_other = dot(features, other[...])
            kv = lax.dot_general(
                keyval[...], features, (((1,), (1,)), ((), ())), preferred_element_type=f32
            )
            for k in range(together):
                dx = step * together + k
                out[dx, :block, :] = q_mine[k * block : (k + 1) * block]
                out[dx, part : part + block, :] = q_other[k * block : (k + 1) * block]
                for core in range(NC):
                    top = core * part + block
                    for side in range(2):
                        first = core * fresh + side * fresh // 2
                        out[dx, top : top + fresh // 2, side * block : (side + 1) * block] = kv[
                            first : first + fresh // 2, k * block : (k + 1) * block
                        ]

    spec = pl.BlockSpec(memory_space=pltpu.VMEM)
    return pl.pallas_call(
        kernel,
        out_shape=jax.ShapeDtypeStruct((NX, 2 * part, columns), f32),
        in_specs=[spec] * (count + 3),
        out_specs=spec,
        scratch_shapes=[pltpu.VMEM((NX * block, 2 * half), bf16)],
        compiler_params=pltpu.CompilerParams(vmem_limit_bytes=32 * 1024 * 1024),
        cost_estimate=pl.CostEstimate(
            flops=8 * NX * block * half * (columns + fresh),
            bytes_accessed=4 * NX * block * half + 8 * half * columns,
            transcendentals=0,
        ),
        name="project",
    )(*messages, w_mine, w_other, w_keyval)


def on_device(
    hidden, norm_gain, w_query, w_keyval, w_out, cache_keys, cache_values, cache_lengths, positions
):
    x, y, z, c = (lax.axis_index(a) for a in "xyzc")
    rows, steps, width = hidden.shape
    tokens = rows * steps
    half = width // 2
    head_cols = w_query.shape[1]
    keyval_cols = w_keyval.shape[2]

    def in_core_order(own, swapped, axis):
        return jnp.where(
            c == 0, jnp.stack([own, swapped], axis=axis), jnp.stack([swapped, own], axis=axis)
        )

    features = hidden.reshape(tokens, width).astype(f32)
    squares = jnp.sum(features * features, axis=-1)
    square_sums = squares + recv(squares, "y", 1) + recv(squares, "y", 2) + recv(squares, "y", 3)
    inverse = lax.rsqrt(square_sums / (width * NY) + norm_epsilon)
    normed = (features * inverse[:, None] * norm_gain.astype(f32)).astype(bf16)
    messages, item_places = gather_rows(jnp.concatenate([normed[:, :half], normed[:, half:]]))

    w_query, w_keyval, w_out, _ = lax.optimization_barrier(
        (w_query, w_keyval, w_out, messages[1])
    )
    w_query_other = recv(w_query, "c", 1)
    w_keyval = w_keyval.transpose(0, 2, 1).reshape(2 * keyval_cols, width)
    w_keyval = jnp.concatenate([w_keyval, recv(w_keyval, "c", 1)])
    w_out = jnp.concatenate([w_out, recv(w_out, "c", 1)])

    places = positions.astype(f32)[:, None] + jnp.arange(steps, dtype=f32)[None, :]
    angles = places.reshape(-1)[:, None] * rope_rates()
    cosine, sine = jnp.cos(angles), jnp.sin(angles)
    cosine = jnp.concatenate([cosine, cosine], axis=1)
    sine = jnp.concatenate([-sine, sine], axis=1)

    partial = project(messages, item_places, w_query, w_query_other, w_keyval)
    block = NZ * tokens

    def block_for(d):
        return lax.dynamic_index_in_dim(partial, (y + d - x + NX) % NX, 0, keepdims=False)

    summed = block_for(0)
    for d in (1, 2, 3):
        summed = summed + recv(block_for(d), "y", -d)
    summed = summed.astype(bf16)
    part = summed.shape[0] // 2
    own, swapped = summed[:part], recv(summed[part:], "c", 1)

    def queries_of(a):
        return a[:block].reshape(NZ, tokens, head_cols)

    def keyvals_of(a):
        a = jnp.concatenate([a[block:, :block], a[block:, block:]])
        return a.T.reshape(NZ, tokens, 2 * keyval_cols)

    back = (NZ - z) % NZ
    q = roll_to(in_core_order(queries_of(own), queries_of(swapped), 1), back)
    kv = roll_to(in_core_order(keyvals_of(own), keyvals_of(swapped), 1), back)
    places_out = 2 * block // TOKENS
    q = q.reshape(places_out, TOKENS, head_cols // HD, HD).transpose(0, 2, 1, 3)
    q = q.reshape(places_out, -1, HD)
    kv = kv.reshape(places_out, 1, -1)
    arrived = lax.all_to_all(
        jnp.concatenate([q, kv], axis=1), ("x", "z", "c"), split_axis=0, concat_axis=0, tiled=True
    )
    q_rows = q.shape[1]
    queries = arrived[:, :q_rows].reshape(-1, HD)
    keyvals = arrived[:, q_rows].reshape(places_out, TOKENS, 2, keyval_cols)
    keyvals = keyvals.transpose(2, 1, 0, 3).reshape(2, TOKENS, KVH, HD)
    fresh_keys = keyvals[0].astype(f32)
    turned_keys = (
        fresh_keys * cosine[:, None] + jnp.roll(fresh_keys, HALF, axis=-1) * sine[:, None]
    ).astype(bf16)
    new = jnp.stack([turned_keys, keyvals[1]]).reshape(2, TOKENS, KVH * HD)
    padded = jnp.pad(new, ((0, 0), (0, 16 - TOKENS), (0, 0)))
    attended = attend(
        queries,
        jnp.tile(cosine, (2, 1)),
        jnp.tile(sine, (2, 1)),
        cache_keys,
        cache_values,
        padded,
        cache_lengths,
    )
    returned = lax.all_to_all(
        attended.reshape(places_out, -1, HD), ("x", "z", "c"), split_axis=0, concat_axis=0, tiled=True
    )
    returned = returned.reshape(places_out, head_cols // HD, TOKENS, HD).transpose(0, 2, 1, 3)
    returned = roll_to(returned.reshape(NZ, NC, tokens, head_cols), z)
    kept = lax.dynamic_index_in_dim(returned, c, 1, keepdims=False)
    got = recv(lax.dynamic_index_in_dim(returned, 1 - c, 1, keepdims=False), "c", 1)
    returned = jnp.concatenate([kept, got], axis=2).reshape(block, 2 * head_cols)
    line = jnp.stack([returned] + [recv(returned, "y", d) for d in (1, 2, 3)])
    new_keyvals = new.reshape(2, TOKENS // steps, steps, KVH * HD)
    line, new_keyvals = lax.optimization_barrier((line, new_keyvals))
    left = jnp.concatenate(
        [
            lax.dynamic_index_in_dim(line, (x + i - y + NX) % NX, 0, keepdims=False)
            for i in range(NX)
        ]
    )
    branch = scatter_rows(dot(left, w_out), tokens)
    return branch.reshape(rows, steps, width), new_keyvals


def solution(mesh):
    fine = Mesh(mesh.devices.reshape(NY, NX, NZ, NC), ("y", "x", "z", "c"))
    gy = ("x", "z", "c")
    everywhere = ("y", "x", "z", "c")
    return jax.shard_map(
        on_device,
        mesh=fine,
        in_specs=(
            P(gy, None, "y"),
            P("y"),
            P("y", gy),
            P(None, "y", gy),
            P(gy, "y"),
            P(everywhere, None, None),
            P(everywhere, None, None),
            P(everywhere),
            P(everywhere),
        ),
        out_specs=(P(gy, None, "y"), P(None, everywhere, None, None)),
        check_vma=False,
    )
```
